32 devices in a mesh: seq: 2 (over y), rows: 16 (over z, x, core).
Axes of the slice: x: 2, y: 2, z: 4, core: 2. Of those that a mesh axis runs over, the one named last changes fastest.
Arguments:
- inputs: bfloat16 [32, 1024, 768], P('rows', 'seq'), may hold values from -6 to 6
- doc_ids: int32 [32, 1024], P('rows', 'seq'), may hold values from 0 to 1023, as said below
- first_gain: float32 [768], replicated, may hold values from 0.1 to 1.9
- first_shift: float32 [768], replicated, may hold values from -3 to 3
- qkv_weight: bfloat16 [768, 2304], replicated, may hold values from -0.21875 to 0.21875
- query_bias: float32 [768], replicated, may hold values from -2 to 2
- value_bias: float32 [768], replicated, may hold values from -2 to 2
- out_weight: bfloat16 [768, 768], replicated, may hold values from -3.5 to 3.5
- out_bias: float32 [768], replicated, may hold values from -3 to 3
- second_gain: float32 [768], replicated, may hold values from 0.1 to 1.9
- second_shift: float32 [768], replicated, may hold values from -3 to 3
- fc_weight: bfloat16 [768, 3072], replicated, may hold values from -0.21875 to 0.21875
- fc_bias: float32 [3072], replicated, may hold values from -2 to 2
- proj_weight: bfloat16 [3072, 768], replicated, may hold values from -0.625 to 0.625
- proj_bias: float32 [768], replicated, may hold values from -3 to 3
- cotangent: bfloat16 [32, 1024, 768], P('rows', 'seq'), may hold values from -6 to 6
Outputs:
- output: bfloat16 [32, 1024, 768], P('rows', 'seq')
- grad_inputs: bfloat16 [32, 1024, 768], P('rows', 'seq')
- grad_first_gain: float32 [768], P('rows')
- grad_first_shift: float32 [768], P('rows')
- grad_qkv_weight: float32 [768, 2304], P('rows')
- grad_query_bias: float32 [768], P('rows')
- grad_value_bias: float32 [768], P('rows')
- grad_out_weight: float32 [768, 768], P('rows')
- grad_out_bias: float32 [768], P('rows')
- grad_second_gain: float32 [768], P('rows')
- grad_second_shift: float32 [768], P('rows')
- grad_fc_weight: float32 [768, 3072], P('rows')
- grad_fc_bias: float32 [3072], P('rows')
- grad_proj_weight: float32 [3072, 768], P('rows')
- grad_proj_bias: float32 [768], P('rows')
The draws below stay inside these ranges and needn't reach their ends.
Inputs may be any that keep to these rules, and one draw needn't show every extreme that they name: `doc_ids`: every document is a run of adjacent tokens of one row, and its tokens share one number that no other document of the row has; the numbers never fall along a row; the first document of every row has the number 0 and the last one 1024 - 1.
All inputs are finite; a program needn't handle non-finite values.
Results may differ from the reference program's by a relative error of at most 0.019.
Values may be sent and summed in bfloat16 or wider, within the bound.
A program may use at most 320 MiB of HBM per device.

```python
import jax
import jax.numpy as jnp
from jax import lax

D = 768
H = 12
HD = 64
FF = 3072
SEQ_LEN = 1024
LAYERS = 12
TOK_DEV = 512
BATCH = 32


def draw_doc_ids(key, part):
    key = jax.random.fold_in(key, 11)
    first_key, last_key, flag_key = jax.random.split(key, 3)
    positions = jnp.arange(SEQ_LEN, dtype=jnp.int32)[None, :]
    first_cut = jax.random.randint(first_key, (BATCH, 1), 1, TOK_DEV)
    last_cut = jax.random.randint(last_key, (BATCH, 1), SEQ_LEN - TOK_DEV + 1, SEQ_LEN)
    start_flags = jax.random.randint(flag_key, (BATCH, SEQ_LEN), 0, 32) == 0
    outside = (positions < first_cut) | (positions > last_cut)
    starts = (start_flags & outside | (positions == first_cut) | (positions == last_cut)) & (positions > 0)
    start_marks = jnp.where(starts, positions, SEQ_LEN).astype(jnp.int32)
    later_marks = jnp.concatenate([start_marks[:, 1:], jnp.full((BATCH, 1), SEQ_LEN, jnp.int32)], axis=1)
    next_start = lax.cummin(later_marks, axis=1, reverse=True)
    seen_starts = jnp.cumsum(starts.astype(jnp.int32), axis=1)
    return jnp.where(seen_starts > 0, next_start - 1, 0).astype(jnp.int32)


def levels(key, dims, cuts, least, high):
    def one(dim, shards_of):
        heights = jax.random.uniform(jax.random.fold_in(jax.random.fold_in(key, 6), dim), (shards_of,), jnp.float32, least / len(cuts), high / len(cuts))
        return jnp.repeat(jnp.exp(heights), dims[dim] // shards_of).reshape((-1,) + (1,) * (len(dims) - dim - 1))

    loudness = one(*cuts[0])
    for cut in cuts[1:]:
        loudness = loudness * one(*cut)
    return loudness


def scatter_about(stream_key, shape, deviation, bound, cuts=(), kind=jnp.bfloat16):
    loudness = levels(stream_key, shape, cuts, -0.22, 0.18) if cuts else 1.0
    result = jax.random.normal(stream_key, shape, jnp.float32) * deviation * loudness
    return jnp.minimum(jnp.maximum(result, -bound), bound).astype(kind)


def setup_inputs(seed: int = 0) -> dict:
    key_list = jax.random.split(jax.random.key(seed), 17)
    return {
        "inputs": scatter_about(key_list[0], (BATCH, SEQ_LEN, D), 1.0, 6.0, ((0, 16), (1, 2))),
        "doc_ids": draw_doc_ids(jax.random.fold_in(key_list[16], 71), 0),
        "first_gain": jnp.clip(1.0 + 0.18 * jax.random.normal(key_list[2], (D,), jnp.float32), 0.1, 1.9),
        "first_shift": scatter_about(key_list[3], (D,), 0.5, 3.0, (), jnp.float32),
        "qkv_weight": scatter_about(key_list[4], (D, 3 * D), D ** -0.5, 0.21875),
        "query_bias": scatter_about(key_list[5], (D,), 0.3, 2.0, (), jnp.float32),
        "value_bias": scatter_about(key_list[6], (D,), 0.3, 2.0, (), jnp.float32),
        "out_weight": scatter_about(key_list[7], (D, D), (max(D // 256, 1)) ** -0.5, 3.5),
        "out_bias": scatter_about(key_list[8], (D,), 0.5, 3.0, (), jnp.float32),
        "second_gain": jnp.clip(1.0 + 0.18 * jax.random.normal(key_list[9], (D,), jnp.float32), 0.1, 1.9),
        "second_shift": scatter_about(key_list[10], (D,), 0.5, 3.0, (), jnp.float32),
        "fc_weight": scatter_about(key_list[11], (D, FF), D ** -0.5, 0.21875),
        "fc_bias": scatter_about(key_list[12], (FF,), 0.3, 2.0, (), jnp.float32),
        "proj_weight": scatter_about(key_list[13], (FF, D), (FF // 32) ** -0.5, 0.625),
        "proj_bias": scatter_about(key_list[14], (D,), 0.5, 3.0, (), jnp.float32),
        "cotangent": scatter_about(key_list[15], (BATCH, SEQ_LEN, D), 1.0, 6.0, ((0, 16), (1, 2))),
    }


epsilon = 1e-05
masked_value = -1e+30

@jax.custom_vjp
def low(v):
    return lax.optimization_barrier(v.astype(jnp.bfloat16)).astype(jnp.float32)

@jax.custom_vjp
def low_back(v):
    return v

def low_keep(v):
    return (low(v), None)

def low_pass(kept, grad):
    return (grad,)

def back_keep(v):
    return (v, None)

def back_low(kept, grad):
    return (low(grad),)
low.defvjp(low_keep, low_pass)
low_back.defvjp(back_keep, back_low)

def layer_norm(values, norm_gain, norm_bias):
    row_mean = lax.optimization_barrier(jnp.mean(values, axis=-1, keepdims=True))
    centred = values - row_mean
    variance = lax.optimization_barrier(jnp.mean(centred * centred, axis=-1, keepdims=True))
    return centred * lax.rsqrt(variance + epsilon) * norm_gain + norm_bias

def product(left_side, right_side):
    return jnp.matmul(left_side, right_side, precision=lax.Precision.HIGHEST)

def attention(query_rows, key_rows, value_rows, group_docs):
    groups, length, model_width = query_rows.shape
    query_heads = query_rows.reshape(groups, length, H, HD)
    key_heads = key_rows.reshape(groups, length, H, HD)
    value_heads = value_rows.reshape(groups, length, H, HD)
    raw_scores = low_back(jnp.einsum('gqhd,gkhd->ghqk', query_heads, key_heads, precision=lax.Precision.HIGHEST))
    positions = jnp.arange(length, dtype=jnp.int32)
    causal = positions[None, :] <= positions[:, None]
    same_doc = group_docs[:, :, None] == group_docs[:, None, :]
    allowed = (causal[None] & same_doc)[:, None]
    scores = jnp.where(allowed, raw_scores * HD ** (-0.5), masked_value)
    row_top = lax.optimization_barrier(jnp.max(scores, axis=-1, keepdims=True))
    weights = jnp.where(allowed, jnp.exp(scores - row_top), 0.0)
    attn_probs = low(weights / lax.optimization_barrier(jnp.sum(weights, axis=-1, keepdims=True)))
    attended = jnp.einsum('ghqk,gkhd->gqhd', attn_probs, value_heads, precision=lax.Precision.HIGHEST)
    return attended.reshape(groups, length, model_width)

def forward(layer_inputs, layer_params, group_docs):
    first_gain, first_shift, qkv_weight, query_bias, value_bias, out_weight, out_bias, second_gain, second_shift, fc_weight, fc_bias, proj_weight, proj_bias = layer_params
    branch_scale = LAYERS ** (-0.5)
    normed_first = low(layer_norm(layer_inputs, first_gain, first_shift))
    bias_row = jnp.concatenate([query_bias, jnp.zeros_like(query_bias), value_bias])
    mixed = low_back(low(product(normed_first, qkv_weight) + bias_row))
    attended = attention(mixed[..., :D], mixed[..., D:2 * D], mixed[..., 2 * D:], group_docs)
    attended_low = low_back(low(attended))
    branch_one = low_back(product(attended_low, out_weight) + out_bias)
    middle = layer_inputs + branch_scale * branch_one
    normed_second = low(layer_norm(middle, second_gain, second_shift))
    hidden = low_back(product(normed_second, fc_weight) + fc_bias)
    activated = low(jax.nn.gelu(hidden, approximate=True))
    branch_two = low_back(product(activated, proj_weight) + proj_bias)
    return middle + branch_scale * branch_two

def reference(inputs, doc_ids, first_gain, first_shift, qkv_weight, query_bias, value_bias, out_weight, out_bias, second_gain, second_shift, fc_weight, fc_bias, proj_weight, proj_bias, cotangent):
    batch_total = inputs.shape[0]
    group_size = 4 if batch_total % 4 == 0 else 1
    group_count = batch_total // group_size
    params = tuple((member.astype(jnp.float32) for member in (first_gain, first_shift, qkv_weight, query_bias, value_bias, out_weight, out_bias, second_gain, second_shift, fc_weight, fc_bias, proj_weight, proj_bias)))
    grouped_inputs = inputs.astype(jnp.float32).reshape(group_count, group_size, SEQ_LEN, D)
    grouped_docs = doc_ids.astype(jnp.int32).reshape(group_count, group_size, SEQ_LEN)
    grouped_cot = cotangent.astype(jnp.float32).reshape(group_count, group_size, SEQ_LEN, D)

    def one_group(running_sums, slices):
        group_inputs, group_docs, group_cot = slices

        def apply_layer(layer_inputs, layer_params):
            return forward(layer_inputs, layer_params, group_docs)
        layer_out, pullback = jax.vjp(apply_layer, group_inputs, params)
        grad_in, grad_params = pullback(group_cot)
        running_sums = jax.tree.map(jnp.add, running_sums, grad_params)
        return (running_sums, (layer_out.astype(jnp.bfloat16), grad_in.astype(jnp.bfloat16)))
    initial = jax.tree.map(jnp.zeros_like, params)
    running_sums, (outputs, grad_inputs) = lax.scan(one_group, initial, (grouped_inputs, grouped_docs, grouped_cot))
    return (outputs.reshape(batch_total, SEQ_LEN, D), grad_inputs.reshape(batch_total, SEQ_LEN, D), running_sums[0], running_sums[1], running_sums[2], running_sums[3], running_sums[4], running_sums[5], running_sums[6], running_sums[7], running_sums[8], running_sums[9], running_sums[10], running_sums[11], running_sums[12])
```

```python
import functools
import math

import jax
import jax.numpy as jnp
from jax import lax
from jax.experimental import pallas as pl
from jax.experimental.pallas import tpu as pltpu
from jax.sharding import PartitionSpec as P

H = 12
HD = 64
LAYERS = 12


epsilon = 1e-05
masked_value = -1e30


def layer_norm(values, norm_gain, norm_bias):
    row_mean = jnp.mean(values, axis=-1, keepdims=True)
    centred = values - row_mean
    variance = jnp.mean(centred * centred, axis=-1, keepdims=True)
    return centred * lax.rsqrt(variance + epsilon) * norm_gain + norm_bias


def gelu_tanh(values):
    return jax.nn.gelu(values, approximate=True)


def matmul_rows(left_side, weight):
    flat_rows = left_side.reshape(-1, left_side.shape[-1])
    result = jnp.dot(flat_rows, weight, preferred_element_type=jnp.float32)
    return result.reshape(left_side.shape[:-1] + (weight.shape[1],))


def back_rows(grads_low, weight):
    flat_rows = grads_low.reshape(-1, grads_low.shape[-1])
    result = jnp.einsum("nm,km->nk", flat_rows, weight, preferred_element_type=jnp.float32)
    return result.reshape(grads_low.shape[:-1] + (weight.shape[0],))


def weight_grad(left_side, right_side):
    left_flat = left_side.reshape(-1, left_side.shape[-1])
    right_flat = right_side.reshape(-1, right_side.shape[-1])
    return jnp.einsum("nk,nm->km", left_flat, right_flat, preferred_element_type=jnp.float32)


def column_sums(values):
    return jnp.sum(values.astype(jnp.float32), axis=(0, 1))


def visible(query_pos, query_doc, key_pos, key_doc):
    causal = key_pos[None, None, :] <= query_pos[None, :, None]
    same_doc = key_doc[:, None, :] == query_doc[:, :, None]
    return (causal & same_doc)[:, None]


def split_heads(kv_part):
    rows_here, key_count = (kv_part.shape[0], kv_part.shape[1])
    model_width = H * HD
    key_heads = kv_part[..., :model_width].reshape(rows_here, key_count, H, HD)
    return (key_heads, rows_here, key_count)


def scaled_scores(query_heads, key_heads, allowed):
    raw_scores = jnp.einsum(
        "rqhd,rkhd->rhqk", query_heads, key_heads, preferred_element_type=jnp.float32
    )
    return jnp.where(allowed, raw_scores * HD ** (-0.5), masked_value)


def guarded(folder, query_pos, query_doc):

    def update(totals, portion, offset):
        doc_part = portion[1]
        early_enough = offset <= query_pos[-1]
        doc_meets = jnp.any(jnp.max(doc_part, axis=1) >= jnp.min(query_doc, axis=1))
        return lax.cond(
            early_enough & doc_meets,
            lambda carried: folder(carried, portion, offset),
            lambda carried: carried,
            totals,
        )

    return update


def stats_update(query_heads, query_pos, query_doc):

    def update(totals, portion, offset):
        running_top, row_mass = totals
        kv_part, doc_part = portion
        key_heads, rows_here, key_count = split_heads(kv_part)
        key_pos = jnp.arange(key_count, dtype=jnp.int32)
        allowed = visible(query_pos, query_doc, key_pos, doc_part)
        scores = scaled_scores(query_heads, key_heads, allowed)
        new_top = jnp.maximum(running_top, jnp.max(scores, axis=-1))
        weights = jnp.where(allowed, jnp.exp(scores - new_top[..., None]), 0.0)
        row_mass = jnp.sum(weights, axis=-1)
        return (new_top, row_mass)

    return guarded(update, query_pos, query_doc)


def output_update(query_heads, query_pos, query_doc, running_top, row_mass):

    def update(totals, portion, offset):
        kv_part, doc_part = portion
        key_heads, rows_here, key_count = split_heads(kv_part)
        value_heads = kv_part[..., H * HD :].reshape(rows_here, key_count, H, HD)
        key_pos = jnp.arange(key_count, dtype=jnp.int32)
        allowed = visible(query_pos, query_doc, key_pos, doc_part)
        scores = scaled_scores(query_heads, key_heads, allowed)
        attn_probs = (
            jnp.where(allowed, jnp.exp(scores - running_top[..., None]), 0.0) / row_mass[..., None]
        )
        result = jnp.einsum(
            "rhqk,rkhd->rqhd",
            attn_probs.astype(jnp.bfloat16),
            value_heads,
            preferred_element_type=jnp.float32,
        )
        return result.reshape(totals.shape)

    return guarded(update, query_pos, query_doc)


def backward_update(
    query_heads, grad_heads, query_pos, query_doc, running_top, row_mass, row_delta
):

    def update(totals, portion, offset):
        grad_query, kv_grads = totals
        kv_part, doc_part = portion
        key_heads, rows_here, key_count = split_heads(kv_part)
        value_heads = kv_part[..., H * HD :].reshape(rows_here, key_count, H, HD)
        key_pos = jnp.arange(key_count, dtype=jnp.int32)
        allowed = visible(query_pos, query_doc, key_pos, doc_part)
        scores = scaled_scores(query_heads, key_heads, allowed)
        attn_probs = (
            jnp.where(allowed, jnp.exp(scores - running_top[..., None]), 0.0) / row_mass[..., None]
        )
        grad_probs = jnp.einsum(
            "rqhd,rkhd->rhqk", grad_heads, value_heads, preferred_element_type=jnp.float32
        )
        grad_scores = (attn_probs * (grad_probs - row_delta[..., None]) * HD ** (-0.5)).astype(
            jnp.bfloat16
        )
        query_part = jnp.einsum(
            "rhqk,rkhd->rqhd", grad_scores, key_heads, preferred_element_type=jnp.float32
        )
        grad_query = query_part.reshape(grad_query.shape)
        key_part = jnp.einsum(
            "rhqk,rqhd->rkhd", grad_scores, query_heads, preferred_element_type=jnp.float32
        )
        value_part = jnp.einsum(
            "rhqk,rqhd->rkhd",
            attn_probs.astype(jnp.bfloat16),
            grad_heads,
            preferred_element_type=jnp.float32,
        )
        piece_grads = jnp.concatenate(
            [
                key_part.reshape(rows_here, key_count, H * HD),
                value_part.reshape(rows_here, key_count, H * HD),
            ],
            axis=-1,
        )
        kv_grads = piece_grads
        return (grad_query, kv_grads)

    return guarded(update, query_pos, query_doc)


BF = jnp.bfloat16
F32 = jnp.float32
NT = (((1,), (1,)), ((), ()))
NN = (((1,), (0,)), ((), ()))
EXP2_SCALE = 0.125 * math.log2(math.e)
QB = 256


def dot(left, right, dims=NN):
    return lax.dot_general(left, right, dims, preferred_element_type=F32)


def build_bias(doc_row, doc_col, bias):
    tokens = bias.shape[0]
    for i in range(tokens // QB):
        seen = (i + 1) * QB
        key = lax.broadcasted_iota(jnp.int32, (seen, QB), 0)
        query = lax.broadcasted_iota(jnp.int32, (seen, QB), 1) + i * QB
        allowed = (key <= query) & (doc_col[0:seen, 0:1] == doc_row[0:1, i * QB : seen])
        bias[0:seen, i * QB : seen] = jnp.where(allowed, 0.0, masked_value)


def half_mask(pair, h):
    lane = lax.broadcasted_iota(jnp.int32, pair.shape, 1)
    return jnp.where((lane < HD) if h == 0 else (lane >= HD), pair, jnp.zeros_like(pair))


def attend_kernel(q_ref, k_ref, v_ref, doc_row, doc_col, o_ref, lse_ref, bias, o_turned):
    @pl.when(pl.program_id(0) == 0)
    def _():
        build_bias(doc_row, doc_col, bias)

    tokens = q_ref.shape[0]
    v_turned = v_ref[...].astype(F32).T.astype(BF)
    queries = [half_mask(q_ref[...], h) for h in range(2)]

    def scores(h, i):
        seen = (i + 1) * QB
        here = slice(i * QB, seen)
        return dot(k_ref[0:seen, :], queries[h][here], NT) * EXP2_SCALE + bias[0:seen, here]

    jobs = [(h, i) for i in range(tokens // QB) for h in range(2)]
    results = {}
    now = scores(*jobs[0])
    for place, (h, i) in enumerate(jobs):
        later = scores(*jobs[place + 1]) if place + 1 < len(jobs) else None
        seen = (i + 1) * QB
        top = jnp.max(now, axis=0, keepdims=True)
        probs = jnp.exp2(now - top)
        mass = jnp.sum(probs, axis=0, keepdims=True)
        part = dot(v_turned[h * HD : (h + 1) * HD, :seen], probs.astype(BF))
        results[h, i] = (part / mass, top + jnp.log2(mass))
        now = later
    for (h, i), (part, lse) in results.items():
        here = slice(i * QB, (i + 1) * QB)
        o_turned[h * HD : (h + 1) * HD, here] = part
        lse_ref[0, h : h + 1, here] = lse
    o_ref[...] = o_turned[...].T.astype(BF)


def attend(mixed, doc_row, doc_col):
    tokens = mixed.shape[0]
    pairs = H // 2
    width = 2 * HD
    part = lambda base: pl.BlockSpec((tokens, width), lambda p: (0, base + p))
    return pl.pallas_call(
        attend_kernel,
        grid=(pairs,),
        out_shape=(
            jax.ShapeDtypeStruct((tokens, H * HD), BF),
            jax.ShapeDtypeStruct((pairs, 2, tokens), F32),
        ),
        in_specs=[
            part(0),
            part(pairs),
            part(2 * pairs),
            pl.BlockSpec((1, tokens), lambda p: (0, 0)),
            pl.BlockSpec((tokens, 1), lambda p: (0, 0)),
        ],
        out_specs=(part(0), pl.BlockSpec((1, 2, tokens), lambda p: (p, 0, 0))),
        scratch_shapes=[pltpu.VMEM((tokens, tokens), F32), pltpu.VMEM((width, tokens), F32)],
        compiler_params=pltpu.CompilerParams(vmem_limit_bytes=50 << 20),
        cost_estimate=pl.CostEstimate(flops=3 << 30, bytes_accessed=6 << 20, transcendentals=8 << 20),
        name="attend",
    )(mixed, mixed, mixed, doc_row, doc_col)


def attend_back_kernel(
    q_ref, k_ref, v_ref, do_ref, o_ref, lse_ref, doc_row, doc_col, dq_ref, dk_ref, dv_ref, bias, dq_turned, dk, dv
):
    @pl.when(pl.program_id(0) == 0)
    def _():
        build_bias(doc_row, doc_col, bias)

    tokens = q_ref.shape[0]
    products = (do_ref[...].astype(F32) * o_ref[...].astype(F32)).T
    k_turned = k_ref[...].astype(F32).T.astype(BF)
    dk[...] = jnp.zeros_like(dk)
    dv[...] = jnp.zeros_like(dv)
    for h in range(2):
        queries = half_mask(q_ref[...], h)
        grads = half_mask(do_ref[...], h)
        delta = jnp.sum(products[h * HD : (h + 1) * HD], axis=0, keepdims=True)
        for i in range(tokens // QB):
            seen = (i + 1) * QB
            here = slice(i * QB, seen)
            scores = dot(k_ref[0:seen, :], queries[here], NT) * EXP2_SCALE + bias[0:seen, here]
            probs = jnp.exp2(scores - lse_ref[0, h : h + 1, here])
            grad_probs = dot(v_ref[0:seen, :], grads[here], NT)
            grad_scores = (probs * (grad_probs - delta[:, here])).astype(BF)
            dv[0:seen, :] += dot(probs.astype(BF), grads[here])
            dk[0:seen, :] += dot(grad_scores, queries[here])
            dq_turned[h * HD : (h + 1) * HD, here] = dot(
                k_turned[h * HD : (h + 1) * HD, :seen], grad_scores
            )
    dq_ref[...] = (dq_turned[...].T * 0.125).astype(BF)
    dk_ref[...] = (dk[...] * 0.125).astype(BF)
    dv_ref[...] = dv[...].astype(BF)


def attend_back(mixed, grad_attended, attended, lse, doc_row, doc_col):
    tokens = mixed.shape[0]
    pairs = H // 2
    width = 2 * HD
    part = lambda base: pl.BlockSpec((tokens, width), lambda p: (0, base + p))
    return pl.pallas_call(
        attend_back_kernel,
        grid=(pairs,),
        out_shape=(jax.ShapeDtypeStruct((tokens, H * HD), BF),) * 3,
        in_specs=[
            part(0),
            part(pairs),
            part(2 * pairs),
            part(0),
            part(0),
            pl.BlockSpec((1, 2, tokens), lambda p: (p, 0, 0)),
            pl.BlockSpec((1, tokens), lambda p: (0, 0)),
            pl.BlockSpec((tokens, 1), lambda p: (0, 0)),
        ],
        out_specs=(part(0),) * 3,
        scratch_shapes=[
            pltpu.VMEM((tokens, tokens), F32),
            pltpu.VMEM((width, tokens), F32),
            pltpu.VMEM((tokens, width), F32),
            pltpu.VMEM((tokens, width), F32),
        ],
        compiler_params=pltpu.CompilerParams(vmem_limit_bytes=50 << 20),
        cost_estimate=pl.CostEstimate(flops=12 << 30, bytes_accessed=12 << 20, transcendentals=8 << 20),
        name="attend_back",
    )(mixed, mixed, mixed, grad_attended, attended, lse, doc_row, doc_col)


def swap_in(halves):
    place = lax.axis_index("seq")
    keep = lax.dynamic_index_in_dim(halves, place, 0, keepdims=False)
    give = lax.dynamic_index_in_dim(halves, 1 - place, 0, keepdims=False)
    got = lax.ppermute(give, "seq", [(0, 1), (1, 0)])
    first = place == 0
    return jnp.concatenate([jnp.where(first, keep, got), jnp.where(first, got, keep)], axis=0)


def swap_out(row):
    place = lax.axis_index("seq")
    tokens = row.shape[0] // 2
    keep = lax.dynamic_slice_in_dim(row, place * tokens, tokens, 0)
    give = lax.dynamic_slice_in_dim(row, (1 - place) * tokens, tokens, 0)
    got = lax.ppermute(give, "seq", [(0, 1), (1, 0)])
    first = place == 0
    return jnp.stack([jnp.where(first, keep, got), jnp.where(first, got, keep)], axis=0)


def local(
    inputs,
    doc_ids,
    first_gain,
    first_shift,
    qkv_weight,
    query_bias,
    value_bias,
    out_weight,
    out_bias,
    second_gain,
    second_shift,
    fc_weight,
    fc_bias,
    proj_weight,
    proj_bias,
    cotangent,
):
    branch_scale = LAYERS ** (-0.5)
    rows_here, tokens_here, model_width = inputs.shape
    seq_count = lax.axis_size("seq")
    seq_place = lax.axis_index("seq")
    query_pos = seq_place * tokens_here + jnp.arange(tokens_here, dtype=jnp.int32)
    residual = inputs.astype(jnp.float32)
    normed_first, first_pull = jax.vjp(layer_norm, residual, first_gain, first_shift)
    normed_first_low = normed_first.astype(jnp.bfloat16)
    bias_row = jnp.concatenate([query_bias, jnp.zeros_like(query_bias), value_bias])
    mixed_proj = (matmul_rows(normed_first_low, qkv_weight) + bias_row).astype(jnp.bfloat16)
    query_heads = mixed_proj[..., :model_width].reshape(rows_here, tokens_here, H, HD)
    key_values = mixed_proj[..., model_width:]
    init_top = jnp.full((rows_here, H, tokens_here), masked_value, jnp.float32)
    init_mass = jnp.zeros((rows_here, H, tokens_here), jnp.float32)
    stats_fold = stats_update(query_heads, query_pos, doc_ids)
    running_top, row_mass = stats_fold(
        (init_top, init_mass),
        (
            lax.all_gather(key_values[..., :model_width], "seq", axis=1, tiled=True),
            lax.all_gather(doc_ids, "seq", axis=1, tiled=True),
        ),
        jnp.int32(0),
    )
    out_fold = output_update(query_heads, query_pos, doc_ids, running_top, row_mass)
    zero_rows = jnp.zeros((rows_here, tokens_here, model_width), jnp.float32)
    attended = out_fold(
        zero_rows,
        (
            lax.all_gather(key_values, "seq", axis=1, tiled=True),
            lax.all_gather(doc_ids, "seq", axis=1, tiled=True),
        ),
        jnp.int32(0),
    )
    attended_low = attended.astype(jnp.bfloat16)
    branch_one = matmul_rows(attended_low, out_weight) + out_bias
    middle = residual + branch_scale * branch_one
    normed_second, second_pull = jax.vjp(layer_norm, middle, second_gain, second_shift)
    normed_second_low = normed_second.astype(jnp.bfloat16)
    hidden = matmul_rows(normed_second_low, fc_weight) + fc_bias
    activated, gelu_pull = jax.vjp(gelu_tanh, hidden)
    activated_low = activated.astype(jnp.bfloat16)
    branch_two = matmul_rows(activated_low, proj_weight) + proj_bias
    output = (middle + branch_scale * branch_two).astype(jnp.bfloat16)
    grad_output = cotangent.astype(jnp.float32)
    grad_branch_two = (branch_scale * grad_output).astype(jnp.bfloat16)
    grad_proj_weight = weight_grad(activated_low, grad_branch_two)
    grad_proj_bias = column_sums(grad_branch_two)
    grad_activated = back_rows(grad_branch_two, proj_weight)
    grad_hidden = gelu_pull(grad_activated)[0].astype(jnp.bfloat16)
    grad_fc_weight = weight_grad(normed_second_low, grad_hidden)
    grad_fc_bias = column_sums(grad_hidden)
    grad_normed_second = back_rows(grad_hidden, fc_weight)
    grad_from_norm, grad_second_gain, grad_second_shift = second_pull(grad_normed_second)
    grad_middle = grad_output + grad_from_norm
    grad_branch_one = (branch_scale * grad_middle).astype(jnp.bfloat16)
    grad_out_weight = weight_grad(attended_low, grad_branch_one)
    grad_out_bias = column_sums(grad_branch_one)
    grad_attended = back_rows(grad_branch_one, out_weight).astype(jnp.bfloat16)
    grad_heads = grad_attended.reshape(rows_here, tokens_here, H, HD)
    row_delta = jnp.einsum(
        "rqhd,rqhd->rhq",
        grad_heads.astype(jnp.float32),
        attended.reshape(rows_here, tokens_here, H, HD),
    )
    back_fold = backward_update(
        query_heads, grad_heads, query_pos, doc_ids, running_top, row_mass, row_delta
    )
    back_initial = (
        jnp.zeros((rows_here, tokens_here, model_width), jnp.float32),
        jnp.zeros((rows_here, tokens_here * seq_count, 2 * model_width), jnp.float32),
    )
    grad_query, kv_grads = back_fold(
        back_initial,
        (
            lax.all_gather(key_values, "seq", axis=1, tiled=True),
            lax.all_gather(doc_ids, "seq", axis=1, tiled=True),
        ),
        jnp.int32(0),
    )
    kv_summed = lax.psum_scatter(
        kv_grads.astype(jnp.bfloat16), "seq", scatter_dimension=1, tiled=True
    )
    grad_mixed = jnp.concatenate([grad_query.astype(jnp.bfloat16), kv_summed], axis=-1)
    grad_qkv_weight = weight_grad(normed_first_low, grad_mixed)
    mixed_sums = column_sums(grad_mixed)
    grad_query_bias = mixed_sums[:model_width]
    grad_value_bias = mixed_sums[2 * model_width :]
    grad_normed_first = back_rows(grad_mixed, qkv_weight)
    grad_from_first, grad_first_gain, grad_first_shift = first_pull(grad_normed_first)
    grad_inputs = (grad_middle + grad_from_first).astype(jnp.bfloat16)
    all_shares = (
        lax.psum_scatter(
            grad_first_gain.astype(jnp.bfloat16), "rows", scatter_dimension=0, tiled=True
        ).astype(jnp.float32),
        lax.psum_scatter(
            grad_first_shift.astype(jnp.bfloat16), "rows", scatter_dimension=0, tiled=True
        ).astype(jnp.float32),
        lax.psum_scatter(
            grad_qkv_weight.astype(jnp.bfloat16), "rows", scatter_dimension=0, tiled=True
        ).astype(jnp.float32),
        lax.psum_scatter(
            grad_query_bias.astype(jnp.bfloat16), "rows", scatter_dimension=0, tiled=True
        ).astype(jnp.float32),
        lax.psum_scatter(
            grad_value_bias.astype(jnp.bfloat16), "rows", scatter_dimension=0, tiled=True
        ).astype(jnp.float32),
        lax.psum_scatter(
            grad_out_weight.astype(jnp.bfloat16), "rows", scatter_dimension=0, tiled=True
        ).astype(jnp.float32),
        lax.psum_scatter(
            grad_out_bias.astype(jnp.bfloat16), "rows", scatter_dimension=0, tiled=True
        ).astype(jnp.float32),
        lax.psum_scatter(
            grad_second_gain.astype(jnp.bfloat16), "rows", scatter_dimension=0, tiled=True
        ).astype(jnp.float32),
        lax.psum_scatter(
            grad_second_shift.astype(jnp.bfloat16), "rows", scatter_dimension=0, tiled=True
        ).astype(jnp.float32),
        lax.psum_scatter(
            grad_fc_weight.astype(jnp.bfloat16), "rows", scatter_dimension=0, tiled=True
        ).astype(jnp.float32),
        lax.psum_scatter(
            grad_fc_bias.astype(jnp.bfloat16), "rows", scatter_dimension=0, tiled=True
        ).astype(jnp.float32),
        lax.psum_scatter(
            grad_proj_weight.astype(jnp.bfloat16), "rows", scatter_dimension=0, tiled=True
        ).astype(jnp.float32),
        lax.psum_scatter(
            grad_proj_bias.astype(jnp.bfloat16), "rows", scatter_dimension=0, tiled=True
        ).astype(jnp.float32),
    )
    (
        grad_first_gain,
        grad_first_shift,
        grad_qkv_weight,
        grad_query_bias,
        grad_value_bias,
        grad_out_weight,
        grad_out_bias,
        grad_second_gain,
        grad_second_shift,
        grad_fc_weight,
        grad_fc_bias,
        grad_proj_weight,
        grad_proj_bias,
    ) = (
        lax.psum(all_shares[0].astype(jnp.bfloat16), "seq").astype(jnp.float32),
        lax.psum(all_shares[1].astype(jnp.bfloat16), "seq").astype(jnp.float32),
        lax.psum(all_shares[2].astype(jnp.bfloat16), "seq").astype(jnp.float32),
        lax.psum(all_shares[3].astype(jnp.bfloat16), "seq").astype(jnp.float32),
        lax.psum(all_shares[4].astype(jnp.bfloat16), "seq").astype(jnp.float32),
        lax.psum(all_shares[5].astype(jnp.bfloat16), "seq").astype(jnp.float32),
        lax.psum(all_shares[6].astype(jnp.bfloat16), "seq").astype(jnp.float32),
        lax.psum(all_shares[7].astype(jnp.bfloat16), "seq").astype(jnp.float32),
        lax.psum(all_shares[8].astype(jnp.bfloat16), "seq").astype(jnp.float32),
        lax.psum(all_shares[9].astype(jnp.bfloat16), "seq").astype(jnp.float32),
        lax.psum(all_shares[10].astype(jnp.bfloat16), "seq").astype(jnp.float32),
        lax.psum(all_shares[11].astype(jnp.bfloat16), "seq").astype(jnp.float32),
        lax.psum(all_shares[12].astype(jnp.bfloat16), "seq").astype(jnp.float32),
    )
    return (
        output,
        grad_inputs,
        grad_first_gain,
        grad_first_shift,
        grad_qkv_weight,
        grad_query_bias,
        grad_value_bias,
        grad_out_weight,
        grad_out_bias,
        grad_second_gain,
        grad_second_shift,
        grad_fc_weight,
        grad_fc_bias,
        grad_proj_weight,
        grad_proj_bias,
    )


def local_rows(
    inputs,
    doc_ids,
    first_gain,
    first_shift,
    qkv_weight,
    query_bias,
    value_bias,
    out_weight,
    out_bias,
    second_gain,
    second_shift,
    fc_weight,
    fc_bias,
    proj_weight,
    proj_bias,
    cotangent,
):
    branch_scale = LAYERS ** (-0.5)
    model_width = inputs.shape[2]
    row_docs = swap_in(doc_ids)
    doc_row, doc_col = row_docs[None, :], row_docs[:, None]
    residual = swap_in(inputs).astype(F32)[None]
    normed_first, first_pull = jax.vjp(layer_norm, residual, first_gain, first_shift)
    normed_first_low = normed_first.astype(BF)
    bias_row = jnp.concatenate([query_bias, jnp.zeros_like(query_bias), value_bias])
    mixed = (matmul_rows(normed_first_low, qkv_weight) + bias_row).astype(BF)[0]
    grad_output_low = swap_in(cotangent)[None]
    attended_low, lse = attend(mixed, doc_row, doc_col)
    attended_low = attended_low[None]
    middle = residual + branch_scale * (matmul_rows(attended_low, out_weight) + out_bias)
    normed_second, second_pull = jax.vjp(layer_norm, middle, second_gain, second_shift)
    normed_second_low = normed_second.astype(BF)
    hidden = matmul_rows(normed_second_low, fc_weight) + fc_bias
    activated, gelu_pull = jax.vjp(gelu_tanh, hidden)
    activated_low = activated.astype(BF)
    branch_two = matmul_rows(activated_low, proj_weight) + proj_bias
    output = swap_out((middle + branch_scale * branch_two).astype(BF)[0])
    grad_output = grad_output_low.astype(F32)
    grad_branch_two = (branch_scale * grad_output).astype(BF)
    grad_proj_weight = weight_grad(activated_low, grad_branch_two)
    grad_hidden = gelu_pull(back_rows(grad_branch_two, proj_weight))[0].astype(BF)
    grad_fc_weight = weight_grad(normed_second_low, grad_hidden)
    grad_from_norm, grad_second_gain, grad_second_shift = second_pull(back_rows(grad_hidden, fc_weight))
    grad_middle = grad_output + grad_from_norm
    grad_branch_one = (branch_scale * grad_middle).astype(BF)
    grad_out_weight = weight_grad(attended_low, grad_branch_one)
    grad_attended = back_rows(grad_branch_one, out_weight).astype(BF)
    grad_mixed = attend_back(mixed, grad_attended[0], attended_low[0], lse, doc_row, doc_col)
    grad_mixed = jnp.concatenate(grad_mixed, axis=-1)[None]
    grad_qkv_weight = weight_grad(normed_first_low, grad_mixed)
    mixed_sums = column_sums(grad_mixed)
    grad_from_first, grad_first_gain, grad_first_shift = first_pull(back_rows(grad_mixed, qkv_weight))
    grad_inputs = swap_out((grad_middle + grad_from_first).astype(BF)[0])
    rows_count = lax.axis_size("rows")
    vectors = (
        grad_first_gain,
        grad_first_shift,
        mixed_sums[:model_width],
        mixed_sums[2 * model_width :],
        column_sums(grad_branch_one),
        grad_second_gain,
        grad_second_shift,
        column_sums(grad_branch_two),
        column_sums(grad_hidden),
    )
    packed = jnp.concatenate([v.reshape(rows_count, -1) for v in vectors], axis=1)
    matrices = (grad_qkv_weight, grad_out_weight, grad_fc_weight, grad_proj_weight, packed)
    shares = [
        lax.psum(lax.psum_scatter(m.astype(BF), "rows", scatter_dimension=0, tiled=True), "seq").astype(F32)
        for m in matrices
    ]
    qkv_share, out_share, fc_share, proj_share, packed_share = shares
    cuts = []
    at = 0
    for v in vectors:
        count = v.shape[0] // rows_count
        cuts.append(packed_share[0, at : at + count])
        at += count
    return (
        output,
        grad_inputs,
        cuts[0],
        cuts[1],
        qkv_share,
        cuts[2],
        cuts[3],
        out_share,
        cuts[4],
        cuts[5],
        cuts[6],
        fc_share,
        cuts[8],
        proj_share,
        cuts[7],
    )


def solution(mesh):
    in_specs = (
        P("rows", "seq", None),
        P("rows", "seq"),
        P(),
        P(),
        P(),
        P(),
        P(),
        P(),
        P(),
        P(),
        P(),
        P(),
        P(),
        P(),
        P(),
        P("rows", "seq", None),
    )
    out_specs = (
        P("rows", "seq", None),
        P("rows", "seq", None),
        P("rows"),
        P("rows"),
        P("rows", None),
        P("rows"),
        P("rows"),
        P("rows", None),
        P("rows"),
        P("rows"),
        P("rows"),
        P("rows", None),
        P("rows"),
        P("rows", None),
        P("rows"),
    )
    sizes = dict(mesh.shape)

    def chosen(inputs, *others):
        whole_rows = sizes["seq"] == 2 and inputs.shape[0] == 2
        return (local_rows if whole_rows else local)(inputs, *others)

    return jax.shard_map(chosen, mesh=mesh, in_specs=in_specs, out_specs=out_specs, check_vma=False)
```

```python
import functools
import math

import jax
import jax.numpy as jnp
from jax import lax
from jax.experimental import pallas as pl
from jax.experimental.pallas import tpu as pltpu
from jax.sharding import PartitionSpec as P

H = 12
HD = 64
LAYERS = 12


epsilon = 1e-05
masked_value = -1e30


def layer_norm(values, norm_gain, norm_bias):
    row_mean = jnp.mean(values, axis=-1, keepdims=True)
    centred = values - row_mean
    variance = jnp.mean(centred * centred, axis=-1, keepdims=True)
    return centred * lax.rsqrt(variance + epsilon) * norm_gain + norm_bias


def gelu_tanh(values):
    return jax.nn.gelu(values, approximate=True)


def matmul_rows(left_side, weight):
    flat_rows = left_side.reshape(-1, left_side.shape[-1])
    result = jnp.dot(flat_rows, weight, preferred_element_type=jnp.float32)
    return result.reshape(left_side.shape[:-1] + (weight.shape[1],))


def back_rows(grads_low, weight):
    flat_rows = grads_low.reshape(-1, grads_low.shape[-1])
    result = jnp.einsum("nm,km->nk", flat_rows, weight, preferred_element_type=jnp.float32)
    return result.reshape(grads_low.shape[:-1] + (weight.shape[0],))


def weight_grad(left_side, right_side):
    left_flat = left_side.reshape(-1, left_side.shape[-1])
    right_flat = right_side.reshape(-1, right_side.shape[-1])
    return jnp.einsum("nk,nm->km", left_flat, right_flat, preferred_element_type=jnp.float32)


def column_sums(values):
    return jnp.sum(values.astype(jnp.float32), axis=(0, 1))


def visible(query_pos, query_doc, key_pos, key_doc):
    causal = key_pos[None, None, :] <= query_pos[None, :, None]
    same_doc = key_doc[:, None, :] == query_doc[:, :, None]
    return (causal & same_doc)[:, None]


def split_heads(kv_part):
    rows_here, key_count = (kv_part.shape[0], kv_part.shape[1])
    model_width = H * HD
    key_heads = kv_part[..., :model_width].reshape(rows_here, key_count, H, HD)
    return (key_heads, rows_here, key_count)


def scaled_scores(query_heads, key_heads, allowed):
    raw_scores = jnp.einsum(
        "rqhd,rkhd->rhqk", query_heads, key_heads, preferred_element_type=jnp.float32
    )
    return jnp.where(allowed, raw_scores * HD ** (-0.5), masked_value)


def guarded(folder, query_pos, query_doc):

    def update(totals, portion, offset):
        doc_part = portion[1]
        early_enough = offset <= query_pos[-1]
        doc_meets = jnp.any(jnp.max(doc_part, axis=1) >= jnp.min(query_doc, axis=1))
        return lax.cond(
            early_enough & doc_meets,
            lambda carried: folder(carried, portion, offset),
            lambda carried: carried,
            totals,
        )

    return update


def stats_update(query_heads, query_pos, query_doc):

    def update(totals, portion, offset):
        running_top, row_mass = totals
        kv_part, doc_part = portion
        key_heads, rows_here, key_count = split_heads(kv_part)
        key_pos = jnp.arange(key_count, dtype=jnp.int32)
        allowed = visible(query_pos, query_doc, key_pos, doc_part)
        scores = scaled_scores(query_heads, key_heads, allowed)
        new_top = jnp.maximum(running_top, jnp.max(scores, axis=-1))
        weights = jnp.where(allowed, jnp.exp(scores - new_top[..., None]), 0.0)
        row_mass = jnp.sum(weights, axis=-1)
        return (new_top, row_mass)

    return guarded(update, query_pos, query_doc)


def output_update(query_heads, query_pos, query_doc, running_top, row_mass):

    def update(totals, portion, offset):
        kv_part, doc_part = portion
        key_heads, rows_here, key_count = split_heads(kv_part)
        value_heads = kv_part[..., H * HD :].reshape(rows_here, key_count, H, HD)
        key_pos = jnp.arange(key_count, dtype=jnp.int32)
        allowed = visible(query_pos, query_doc, key_pos, doc_part)
        scores = scaled_scores(query_heads, key_heads, allowed)
        attn_probs = (
            jnp.where(allowed, jnp.exp(scores - running_top[..., None]), 0.0) / row_mass[..., None]
        )
        result = jnp.einsum(
            "rhqk,rkhd->rqhd",
            attn_probs.astype(jnp.bfloat16),
            value_heads,
            preferred_element_type=jnp.float32,
        )
        return result.reshape(totals.shape)

    return guarded(update, query_pos, query_doc)


def backward_update(
    query_heads, grad_heads, query_pos, query_doc, running_top, row_mass, row_delta
):

    def update(totals, portion, offset):
        grad_query, kv_grads = totals
        kv_part, doc_part = portion
        key_heads, rows_here, key_count = split_heads(kv_part)
        value_heads = kv_part[..., H * HD :].reshape(rows_here, key_count, H, HD)
        key_pos = jnp.arange(key_count, dtype=jnp.int32)
        allowed = visible(query_pos, query_doc, key_pos, doc_part)
        scores = scaled_scores(query_heads, key_heads, allowed)
        attn_probs = (
            jnp.where(allowed, jnp.exp(scores - running_top[..., None]), 0.0) / row_mass[..., None]
        )
        grad_probs = jnp.einsum(
            "rqhd,rkhd->rhqk", grad_heads, value_heads, preferred_element_type=jnp.float32
        )
        grad_scores = (attn_probs * (grad_probs - row_delta[..., None]) * HD ** (-0.5)).astype(
            jnp.bfloat16
        )
        query_part = jnp.einsum(
            "rhqk,rkhd->rqhd", grad_scores, key_heads, preferred_element_type=jnp.float32
        )
        grad_query = query_part.reshape(grad_query.shape)
        key_part = jnp.einsum(
            "rhqk,rqhd->rkhd", grad_scores, query_heads, preferred_element_type=jnp.float32
        )
        value_part = jnp.einsum(
            "rhqk,rqhd->rkhd",
            attn_probs.astype(jnp.bfloat16),
            grad_heads,
            preferred_element_type=jnp.float32,
        )
        piece_grads = jnp.concatenate(
            [
                key_part.reshape(rows_here, key_count, H * HD),
                value_part.reshape(rows_here, key_count, H * HD),
            ],
            axis=-1,
        )
        kv_grads = piece_grads
        return (grad_query, kv_grads)

    return guarded(update, query_pos, query_doc)


BF=jnp.bfloat16; F32=jnp.float32
NT=(((1,),(1,)),((),()))
NN=(((1,),(0,)),((),()))
C2=0.125*math.log2(math.e)
QB=256
def dot(a,b,dn=NN): return lax.dot_general(a,b,dn,preferred_element_type=F32)
def build_bias(docr, docc, bias):
    T=bias.shape[0]
    for i in range(T//QB):
        kk=(i+1)*QB
        key=lax.broadcasted_iota(jnp.int32,(kk,QB),0); qry=lax.broadcasted_iota(jnp.int32,(kk,QB),1)+i*QB
        ok=(key<=qry)&(docc[0:kk,0:1]==docr[0:1,i*QB:(i+1)*QB])
        bias[0:kk,i*QB:(i+1)*QB]=jnp.where(ok,0.0,-1e30)
def half_mask(x,h):
    lane=lax.broadcasted_iota(jnp.int32,x.shape,1)
    return jnp.where((lane<64) if h==0 else (lane>=64), x, jnp.zeros_like(x))
def attend_kernel(q_ref, k_ref, v_ref, doc_row, doc_col, o_ref, lse_ref, bias, o_turned):
    @pl.when(pl.program_id(0) == 0)
    def _():
        build_bias(doc_row, doc_col, bias)

    tokens = q_ref.shape[0]
    v_turned = v_ref[...].astype(F32).T.astype(BF)
    queries = [half_mask(q_ref[...], h) for h in range(2)]

    def scores(h, i):
        seen = (i + 1) * QB
        here = slice(i * QB, seen)
        return dot(k_ref[0:seen, :], queries[h][here], NT) * C2 + bias[0:seen, here]

    jobs = [(h, i) for i in range(tokens // QB) for h in range(2)]
    results = {}
    now = scores(*jobs[0])
    for place, (h, i) in enumerate(jobs):
        later = scores(*jobs[place + 1]) if place + 1 < len(jobs) else None
        seen = (i + 1) * QB
        top = jnp.max(now, axis=0, keepdims=True)
        probs = jnp.exp2(now - top)
        mass = jnp.sum(probs, axis=0, keepdims=True)
        part = dot(v_turned[h * HD : (h + 1) * HD, :seen], probs.astype(BF))
        results[h, i] = (part / mass, top + jnp.log2(mass))
        now = later
    for (h, i), (part, lse) in results.items():
        here = slice(i * QB, (i + 1) * QB)
        o_turned[h * HD : (h + 1) * HD, here] = part
        lse_ref[0, h : h + 1, here] = lse
    o_ref[...] = o_turned[...].T.astype(BF)


def attend(mixed, doc_row, doc_col):
    tokens = mixed.shape[0]
    pairs = H // 2
    width = 2 * HD
    part = lambda base: pl.BlockSpec((tokens, width), lambda p: (0, base + p))
    return pl.pallas_call(
        attend_kernel,
        grid=(pairs,),
        out_shape=(
            jax.ShapeDtypeStruct((tokens, H * HD), BF),
            jax.ShapeDtypeStruct((pairs, 2, tokens), F32),
        ),
        in_specs=[
            part(0),
            part(pairs),
            part(2 * pairs),
            pl.BlockSpec((1, tokens), lambda p: (0, 0)),
            pl.BlockSpec((tokens, 1), lambda p: (0, 0)),
        ],
        out_specs=(part(0), pl.BlockSpec((1, 2, tokens), lambda p: (p, 0, 0))),
        scratch_shapes=[pltpu.VMEM((tokens, tokens), F32), pltpu.VMEM((width, tokens), F32)],
        compiler_params=pltpu.CompilerParams(vmem_limit_bytes=50 << 20),
        cost_estimate=pl.CostEstimate(flops=3 << 30, bytes_accessed=6 << 20, transcendentals=8 << 20),
        name="attend",
    )(mixed, mixed, mixed, doc_row, doc_col)


def swap_in(halves):
    place = lax.axis_index("seq")
    keep = lax.dynamic_index_in_dim(halves, place, 0, keepdims=False)
    give = lax.dynamic_index_in_dim(halves, 1 - place, 0, keepdims=False)
    got = lax.ppermute(give, "seq", [(0, 1), (1, 0)])
    first = place == 0
    return jnp.concatenate([jnp.where(first, keep, got), jnp.where(first, got, keep)], axis=0)


TN=(((0,),(0,)),((),()))
D=768
SC=12**-0.5
EPS=1e-5
G0=math.sqrt(2/math.pi); G1=0.044715
TB=256
def ln_stats(x):
    mean=jnp.mean(x,axis=-1,keepdims=True); c=x-mean
    var=jnp.mean(c*c,axis=-1,keepdims=True)
    r=lax.rsqrt(var+EPS)
    return c*r, r
def step_first(x_ref,att_ref,cot_ref,outw_ref,outb,gain,shift,mid,n2,gb2,b2,e):
    T=mid.shape[0]
    for t in range(0,T,TB):
        sl=slice(t,t+TB)
        m=x_ref[sl].astype(F32)+(dot(att_ref[sl],outw_ref[...])+outb[...])*SC
        mid[sl]=m
        xh,_=ln_stats(m)
        n2[sl]=(xh*gain[...]+shift[...]).astype(BF)
        gb2[sl]=(cot_ref[sl].astype(F32)*SC).astype(BF)
        b2[sl]=jnp.zeros((TB,D),F32); e[sl]=jnp.zeros((TB,D),F32)
def gelu_both(h):
    h2=h*h
    t=jnp.tanh(h*(G0+(G0*G1)*h2))
    half=0.5*(1+t)
    act=h*half
    dg=half+act*(1-t)*(G0+(3*G0*G1)*h2)
    return act,dg
def step_ff(j,fcw,fcb,projw,n2,gb2,acts,dhs,b2,e,gfc,gproj,gfcb):
    T=n2.shape[0]
    cs=jnp.zeros((1,fcw.shape[1]),F32)
    blocks=[slice(t,t+TB) for t in range(0,T,TB)]
    first=lambda sl:(dot(n2[sl],fcw[...])+fcb[...], dot(gb2[sl],projw[...],NT))
    now=first(blocks[0])
    for k,sl in enumerate(blocks):
        later=first(blocks[k+1]) if k+1<len(blocks) else None
        h,dA=now
        act,dg=gelu_both(h)
        ab=act.astype(BF); acts[sl]=ab
        dh=(dA*dg).astype(BF); dhs[sl]=dh
        cs=cs+jnp.sum(dh.astype(F32),axis=0,keepdims=True)
        b2[sl]+=dot(ab,projw[...])
        e[sl]+=dot(dh,fcw[...],NT)
        now=later
    gfcb[...]=cs
    gfc(dot(n2[...],dhs[...],TN).astype(BF))
    gproj(dot(acts[...],gb2[...],TN).astype(BF))
def step_after(cot_ref,att_ref,outw_ref,projb,gain,mid,b2,e,gb2,out,gb1,do,gout,vecs):
    T=mid.shape[0]
    z=jnp.zeros((1,D),F32); sg=z; ss=z; sb1=z; sb2=z
    for t in range(0,T,TB):
        sl=slice(t,t+TB)
        m=mid[sl]
        out[sl]=(m+(b2[sl]+projb[...])*SC).astype(BF)
        xh,r=ln_stats(m)
        ee=e[sl]
        sg=sg+jnp.sum(ee*xh,axis=0,keepdims=True); ss=ss+jnp.sum(ee,axis=0,keepdims=True)
        g=ee*gain[...]
        gm=cot_ref[sl].astype(F32)+r*(g-jnp.mean(g,axis=-1,keepdims=True)-xh*jnp.mean(g*xh,axis=-1,keepdims=True))
        mid[sl]=gm
        b1=(gm*SC).astype(BF); gb1[sl]=b1
        sb1=sb1+jnp.sum(b1.astype(F32),axis=0,keepdims=True); sb2=sb2+jnp.sum(gb2[sl].astype(F32),axis=0,keepdims=True)
        do[sl]=dot(b1,outw_ref[...],NT).astype(BF)
    gout(dot(att_ref[...],gb1[...],TN).astype(BF))
    for k,v in enumerate((sg,ss,sb1,sb2)): vecs[k:k+1,:]=v
MESH=pl.DeviceIdType.MESH
NB=48
def add_low(a,b): return (a.astype(F32)+b.astype(F32)).astype(BF)
class Sums:
    def __init__(self,refs,sems,outs):
        (self.gf,self.gp,self.rf,self.rp,self.a,self.ap,self.xb,self.xp,self.z1,self.z1p,self.z2,self.z2p,self.yb,self.yp,self.vs,self.vr)=refs
        (self.cs,self.cr,self.credit,self.xs,self.xr,self.z1s,self.z1r,self.z2s,self.z2r,self.ys,self.yr,self.vss,self.vsr)=sems
        self.share_f,self.share_p=outs
        self.s=lax.axis_index("seq"); r=lax.axis_index("rows"); self.r=r
        self.core=lax.rem(r,2); self.x=lax.rem(r//2,2); self.zl=lax.rem(r//4,2); self.zh=r//8
        flip=lambda d,bit:(self.s, r+d-2*d*bit)
        self.peer=dict(c=flip(1,self.core),x=flip(2,self.x),z1=flip(4,self.zl),z2=flip(8,self.zh),y=(1-self.s,r))
    def barrier(self):
        bar=pltpu.get_barrier_semaphore()
        for d in self.peer.values(): pl.semaphore_signal(bar,inc=1,device_id=d,device_id_type=MESH)
        pl.semaphore_wait(bar,len(self.peer))
    def copy(self,src,dst,ss,rs,to):
        return pltpu.make_async_remote_copy(src_ref=src,dst_ref=dst,send_sem=ss,recv_sem=rs,device_id=self.peer[to],device_id_type=MESH)
    def c_copy(self,kind):
        if kind=="f": return [self.copy(self.gf.at[:,1-self.core],self.rf,self.cs.at[0],self.cr.at[0],"c")]
        return [self.copy(self.gp.at[x,1-self.core],self.rp.at[:,x],self.cs.at[1+x],self.cr.at[1+x],"c") for x in range(2)]
    def c_start(self,kind,first):
        k=0 if kind=="f" else 1
        @pl.when(jnp.logical_not(first))
        def _(): pl.semaphore_wait(self.credit.at[k],1)
        for c in self.c_copy(kind): c.start()
    def c_finish(self,kind,u,last):
        for c in self.c_copy(kind): c.wait()
        if kind=="f":
            for i in range(8):
                zh,zl,x=i//4,(i//2)%2,i%2
                self.a[u,zh,zl,x]=add_low(self.gf[i,self.core],self.rf[i])
        else:
            for t in range(4):
                for x in range(2):
                    self.ap[u//2,lax.rem(u,2),t,x]=add_low(self.gp[x,self.core,t],self.rp[t,x])
        @pl.when(jnp.logical_not(last))
        def _(): pl.semaphore_signal(self.credit.at[0 if kind=="f" else 1],inc=1,device_id=self.peer["c"],device_id_type=MESH)
        self.x_copy(kind,u).start()
    def x_copy(self,kind,u):
        if kind=="f": return self.copy(self.a.at[u,:,:,1-self.x],self.xb.at[u],self.xs.at[u],self.xr.at[u],"x")
        return self.copy(self.ap.at[u//2,lax.rem(u,2),:,1-self.x],self.xp.at[u],self.xs.at[8+u],self.xr.at[8+u],"x")
    def x_finish(self,kind,u):
        self.x_copy(kind,u).wait_recv()
        if kind=="f":
            for zh in range(2):
                for zl in range(2):
                    self.a[u,zh,zl,self.x]=add_low(self.a[u,zh,zl,self.x],self.xb[u,zh,zl])
            self.z1_copy(kind,u).start()
        else:
            for t in range(4):
                self.ap[u//2,u%2,t,self.x]=add_low(self.ap[u//2,u%2,t,self.x],self.xp[u,t])
    def z1_copy(self,kind,u):
        if kind=="f": return self.copy(self.a.at[u,:,1-self.zl,self.x],self.z1.at[u],self.z1s.at[u],self.z1r.at[u],"z1")
        return self.copy(self.ap.at[:,1-self.zl,u,self.x],self.z1p.at[u],self.z1s.at[8+u],self.z1r.at[8+u],"z1")
    def z1_finish(self,kind,u):
        self.z1_copy(kind,u).wait_recv()
        for zh in range(2):
            if kind=="f": self.a[u,zh,self.zl,self.x]=add_low(self.a[u,zh,self.zl,self.x],self.z1[u,zh])
            else: self.ap[zh,self.zl,u,self.x]=add_low(self.ap[zh,self.zl,u,self.x],self.z1p[u,zh])
        self.z2_copy(kind,u).start()
    def z2_copy(self,kind,u):
        if kind=="f": return self.copy(self.a.at[u,1-self.zh,self.zl,self.x],self.z2.at[u],self.z2s.at[u],self.z2r.at[u],"z2")
        return self.copy(self.ap.at[1-self.zh,self.zl,u,self.x],self.z2p.at[u],self.z2s.at[8+u],self.z2r.at[8+u],"z2")
    def mine(self,kind,u):
        return (self.a if kind=="f" else self.ap),((u,self.zh,self.zl,self.x) if kind=="f" else (self.zh,self.zl,u,self.x))
    def z2_finish(self,kind,u):
        self.z2_copy(kind,u).wait_recv()
        ref,at=self.mine(kind,u)
        ref[at]=add_low(ref[at],(self.z2 if kind=="f" else self.z2p)[u])
        self.y_copy(kind,u).start()
    def y_copy(self,kind,u):
        ref,at=self.mine(kind,u)
        k=u if kind=="f" else 8+u
        return self.copy(ref.at[at],(self.yb if kind=="f" else self.yp).at[u],self.ys.at[k],self.yr.at[k],"y")
    def y_finish(self,kind,u):
        self.y_copy(kind,u).wait_recv()
        ref,at=self.mine(kind,u)
        total=ref[at].astype(F32)+(self.yb if kind=="f" else self.yp)[u].astype(F32)
        if kind=="f": self.share_f[u]=total
        else: self.share_p[u]=total
    def wait_sends(self,kind,u):
        for c in (self.x_copy,self.z1_copy,self.z2_copy,self.y_copy): c(kind,u).wait_send()
    def v_copy(self,k):
        return self.copy(self.vs.at[k],self.vr.at[k],self.vss.at[k],self.vsr.at[k],("c","x","z1","z2","y")[k])
    def v_finish(self,k):
        self.v_copy(k).wait()
        self.vs[k+1]=self.vs[k]+self.vr[k]
        if k<4: self.v_copy(k+1).start()

def attn_pair(q_ref,k_ref,v_ref,do,o,lse_ref,bias,dqT,dk,dv,put):
    T=q_ref.shape[0]
    prod=(do.astype(F32)*o.astype(F32)).T
    kT=k_ref[...].astype(F32).T.astype(BF)
    dk[...]=jnp.zeros_like(dk); dv[...]=jnp.zeros_like(dv)
    for h in range(2):
        qh=half_mask(q_ref[...],h); doh=half_mask(do,h)
        delta=jnp.sum(prod[h*64:(h+1)*64],axis=0,keepdims=True)
        for i in range(T//QB):
            kk=(i+1)*QB; sl=slice(i*QB,kk); b0=i*(i+1)//2*QB
            s=dot(k_ref[0:kk,:],qh[sl],NT)*C2+bias[b0:b0+kk,:]
            p=jnp.exp2(s-lse_ref[0,h:h+1,sl])
            dp=dot(v_ref[0:kk,:],doh[sl],NT)
            ds=(p*(dp-delta[:,sl])).astype(BF)
            dv[0:kk,:]+=dot(p.astype(BF),doh[sl])
            dk[0:kk,:]+=dot(ds,qh[sl])
            dqT[h*64:(h+1)*64,sl]=dot(kT[h*64:(h+1)*64,:kk],ds)
    put(0,(dqT[...].T*0.125).astype(BF))
    put(1,(dk[...]*0.125).astype(BF))
    put(2,dv[...].astype(BF))
def build_bias_tri(docr,docc,bias,T):
    for i in range(T//QB):
        kk=(i+1)*QB; b0=i*(i+1)//2*QB
        key=lax.broadcasted_iota(jnp.int32,(kk,QB),0); qry=lax.broadcasted_iota(jnp.int32,(kk,QB),1)+i*QB
        ok=(key<=qry)&(docc[0:kk,0:1]==docr[0:1,i*QB:(i+1)*QB])
        bias[b0:b0+kk,:]=jnp.where(ok,0.0,-1e30)
NSTEP=12
def back_kernel(flags,*refs):
    (x,att,cot,outw,fcw,projw,q_ref,k_ref,v_ref,lse_ref,wq,wk,wv,docr,docc,vec_in,fcb,
     out_hbm,gin_hbm,share_f,share_p,vec_out,
     n2,gb2,acts,dhs,b2,e,mid,bias,dqT,dk,dv,fcbs,vecs,
     *rest)=refs
    nsum=16
    S=Sums(rest[:nsum],rest[nsum:nsum+13],(share_f,share_p))
    swap_s,swap_r,loc=rest[nsum+13:]
    T=mid.shape[0]; half=T//2
    step=pl.program_id(0)
    row=lambda k: vec_in.at[k:k+1]
    OUTB,G2,S2,PB,G1_,S1_=range(6)
    comm="r" in flags; comp="c" in flags
    place=S.s
    def swap(src,dst,k):
        return keep_copy(src,dst,k),give_copy(src,dst,k)
    def keep_copy(src,dst,k):
        return pltpu.make_async_copy(src.at[pl.ds(place*half,half)],dst.at[place],loc.at[k])
    def give_copy(src,dst,k):
        return S.copy(src.at[pl.ds((1-place)*half,half)],dst.at[place],swap_s.at[k],swap_r.at[k],"y")
    def at(k,*fs):
        @pl.when(step==k)
        def _():
            for f in fs: f()
    f_=lambda name,u: (lambda: getattr(S,name+"_finish")("f",u))
    p_=lambda name,u: (lambda: getattr(S,name+"_finish")("p",u))
    gf2=lambda val: S.gf.__setitem__(Ellipsis,val.reshape(8,2,NB,D))
    gp2=lambda val: S.gp.__setitem__(Ellipsis,val.reshape(2,2,4,NB,D))
    @pl.when(step==0)
    def _():
        if comm: S.barrier()
        step_first(x,att,cot,outw,row(OUTB),row(G2),row(S2),mid,n2,gb2,b2,e)
    if comm:
        at(1,lambda:S.c_finish("p",0,False))
        at(2,lambda:S.c_finish("p",1,False),f_("x",0))
        at(3,lambda:S.c_finish("p",2,False),p_("x",0),f_("x",1),f_("z1",0))
        at(4,lambda:S.c_finish("p",3,True),p_("x",1),f_("z1",1),f_("z2",0))
        at(5,f_("x",2),f_("z2",1),f_("y",0))
        at(6,p_("x",2),f_("z1",2),f_("y",1))
        at(7,f_("x",3),f_("z2",2))
        at(8,f_("z1",3),f_("y",2))
        def pz():
            S.x_finish("p",3)
            for t in range(4): S.z1_copy("p",t).start()
        at(9,pz,f_("z2",3))
        at(10,f_("x",4),f_("y",3),p_("z1",0),p_("z1",1))
        at(11,f_("x",5),f_("z1",4),p_("z1",2),p_("z1",3),p_("z2",0),p_("z2",1))
    @pl.when(step<4)
    def _():
        def gfc(val):
            gf2(val)
            if comm: S.c_start("f",step==0)
        def gproj(val):
            gp2(val)
            if comm: S.c_start("p",step==0)
        if comp: step_ff(step,fcw,fcb,projw,n2,gb2,acts,dhs,b2,e,gfc,gproj,fcbs.at[pl.ds(step,1)])
        elif comm: S.c_start("f",step==0); S.c_start("p",step==0)
        if comm: S.c_finish("f",step,False)
    @pl.when(step==4)
    def _():
        def gout(val):
            gf2(val)
            if comm: S.c_start("f",False)
        if comp:
            step_after(cot,att,outw,row(PB),row(G2),mid,b2,e,gb2,dhs,n2,acts,gout,vecs)
        elif comm: S.c_start("f",False)
        if comm:
            for c in swap(dhs,out_hbm,0): c.start()
        if comp:
            build_bias_tri(docr,docc,bias,T)
            for t in range(0,T,TB):
                sl=slice(t,t+TB)
                xh,_=ln_stats(x[sl].astype(F32)); gb2[sl]=(xh*row(G1_)[...]+row(S1_)[...]).astype(BF)
                b2[sl]=jnp.zeros((TB,D),F32)
        if comm: S.c_finish("f",4,False)
    @pl.when((step>=5)&(step<11))
    def _():
        p=step-5; par=lax.rem(p,2); m=p//2
        cols=pl.ds(pl.multiple_of(p*128,128),128)
        def put(part,val):
            n2[:,pl.ds(pl.multiple_of(part*256+par*128,128),128)]=val
            if part!=1:
                vecs[pl.ds(6+part//2,1),cols]=jnp.sum(val.astype(F32),axis=0,keepdims=True)
        if comp: attn_pair(q_ref,k_ref,v_ref,acts[:,cols],att[:,cols],lse_ref,bias,dqT,dk,dv,put)
        @pl.when(par==1)
        def _():
            if comp:
                gf2(dot(gb2[...],n2[...],TN).astype(BF))
            if comm: S.c_start("f",False)
            if comp:
                for t in range(0,T,TB):
                    sl=slice(t,t+TB)
                    b2[sl]+=dot(n2[sl,0:256],wq[...],NT)+dot(n2[sl,256:512],wk[...],NT)+dot(n2[sl,512:768],wv[...],NT)
            if comm: S.c_finish("f",5+m,m==2)
    @pl.when(step==11)
    def _():
        if comm:
            for c in swap(dhs,out_hbm,0): c.wait()
        if comp:
            z=jnp.zeros((1,D),F32)
            vecs[4:6,:]=jnp.zeros((2,D),F32)
            def tok(sl):
                xh,r=ln_stats(x[sl].astype(F32)); ee=b2[sl]
                vecs[4:5,:]+=jnp.sum(ee*xh,axis=0,keepdims=True); vecs[5:6,:]+=jnp.sum(ee,axis=0,keepdims=True)
                g=ee*row(G1_)[...]
                dhs[sl]=(mid[sl]+r*(g-jnp.mean(g,axis=-1,keepdims=True)-xh*jnp.mean(g*xh,axis=-1,keepdims=True))).astype(BF)
            for part in (1-place,place):
                for t in range(0,half,TB):
                    tok(pl.ds(pl.multiple_of(part*half+t,TB),TB))
                if comm:
                    (give_copy if part is not place else keep_copy)(dhs,gin_hbm,1).start()
        elif comm:
            for c in swap(dhs,gin_hbm,1): c.start()
        if comm:
            S.vs[0,0:8]=vecs[...]; S.vs[0,8:12]=fcbs[...]; S.vs[0,12:16]=jnp.zeros((4,D),F32)
            S.v_copy(0).start()
            order=[f_("z1",5),f_("z2",4),lambda:S.v_finish(0),p_("z2",2),p_("z2",3),p_("y",0),p_("y",1),f_("x",6),lambda:S.v_finish(1),f_("z2",5),f_("z1",6),f_("y",4),lambda:S.v_finish(2),
              f_("x",7),f_("z2",6),f_("y",5),lambda:S.v_finish(3),f_("z1",7),p_("y",2),p_("y",3),f_("y",6),f_("z2",7),lambda:S.v_finish(4),f_("y",7)]
            for f in order: f()
            vecs_out=S.vs[5]
            for u in range(8): S.wait_sends("f",u)
            for u in range(4):
                S.wait_sends("p",u)
            for c in swap(dhs,gin_hbm,1): c.wait()
            vec_out[...]=vecs_out
def back(flags,x,att,cot,mixed,lse,docr,docc,outw,fcw,projw,qkvw,vec_in,fcb):
    T=x.shape[0]
    once=pl.Buffered(1)
    full=lambda a,b: pl.BlockSpec((a,b),lambda s:(0,0),pipeline_mode=once)
    j=lambda s: jnp.minimum(s,3)
    p=lambda s: jnp.clip(s-5,0,5)
    m=lambda s: jnp.clip(s-5,0,5)//2
    S=jax.ShapeDtypeStruct
    V=pltpu.VMEM
    return pl.pallas_call(functools.partial(back_kernel,flags),grid=(NSTEP,),
      in_specs=[full(T,D),full(T,D),full(T,D),full(D,D),pl.BlockSpec((D,D),lambda s:(0,j(s))),pl.BlockSpec((D,D),lambda s:(j(s),0)),
        pl.BlockSpec((T,128),lambda s:(0,p(s))),pl.BlockSpec((T,128),lambda s:(0,6+p(s))),pl.BlockSpec((T,128),lambda s:(0,12+p(s))),pl.BlockSpec((1,2,T),lambda s:(p(s),0,0)),
        pl.BlockSpec((D,256),lambda s:(0,m(s))),pl.BlockSpec((D,256),lambda s:(0,3+m(s))),pl.BlockSpec((D,256),lambda s:(0,6+m(s))),
        full(1,T),full(T,1),full(8,D),pl.BlockSpec((1,D),lambda s:(0,j(s)))],
      out_shape=(S((2,T//2,D),BF),S((2,T//2,D),BF),S((8,NB,D),F32),S((4,NB,D),F32),S((16,D),F32)),
      out_specs=(pl.BlockSpec(memory_space=pl.ANY),pl.BlockSpec(memory_space=pl.ANY),pl.BlockSpec((8,NB,D),lambda s:(0,0,0),pipeline_mode=once),pl.BlockSpec((4,NB,D),lambda s:(0,0,0),pipeline_mode=once),pl.BlockSpec((16,D),lambda s:(0,0),pipeline_mode=once)),
      scratch_shapes=[V((T,D),BF)]*4+[V((T,D),F32)]*3+[V((10*QB,QB),F32),V((128,T),F32),V((T,128),F32),V((T,128),F32),V((4,D),F32),V((8,D),F32)]
        +[V((8,2,NB,D),BF),V((2,2,4,NB,D),BF),V((8,NB,D),BF),V((4,2,NB,D),BF),V((8,2,2,2,NB,D),BF),V((2,2,4,2,NB,D),BF),V((8,2,2,NB,D),BF),V((4,4,NB,D),BF),
          V((8,2,NB,D),BF),V((4,2,NB,D),BF),V((8,NB,D),BF),V((4,NB,D),BF),V((8,NB,D),BF),V((4,NB,D),BF),V((6,16,D),F32),V((5,16,D),F32)]
        +[pltpu.SemaphoreType.DMA((3,)),pltpu.SemaphoreType.DMA((3,)),pltpu.SemaphoreType.REGULAR((2,))]+[pltpu.SemaphoreType.DMA((12,))]*8+[pltpu.SemaphoreType.DMA((5,))]*2
        +[pltpu.SemaphoreType.DMA((2,))]*3,
      compiler_params=pltpu.CompilerParams(vmem_limit_bytes=64<<20,collective_id=1,has_side_effects=True,dimension_semantics=("arbitrary",)),name="back_"+flags)(x,att,cot,outw,fcw,projw,mixed,mixed,mixed,lse,qkvw,qkvw,qkvw,docr,docc,vec_in,fcb)


def local(
    inputs,
    doc_ids,
    first_gain,
    first_shift,
    qkv_weight,
    query_bias,
    value_bias,
    out_weight,
    out_bias,
    second_gain,
    second_shift,
    fc_weight,
    fc_bias,
    proj_weight,
    proj_bias,
    cotangent,
):
    branch_scale = LAYERS ** (-0.5)
    rows_here, tokens_here, model_width = inputs.shape
    seq_count = lax.axis_size("seq")
    seq_place = lax.axis_index("seq")
    query_pos = seq_place * tokens_here + jnp.arange(tokens_here, dtype=jnp.int32)
    residual = inputs.astype(jnp.float32)
    normed_first, first_pull = jax.vjp(layer_norm, residual, first_gain, first_shift)
    normed_first_low = normed_first.astype(jnp.bfloat16)
    bias_row = jnp.concatenate([query_bias, jnp.zeros_like(query_bias), value_bias])
    mixed_proj = (matmul_rows(normed_first_low, qkv_weight) + bias_row).astype(jnp.bfloat16)
    query_heads = mixed_proj[..., :model_width].reshape(rows_here, tokens_here, H, HD)
    key_values = mixed_proj[..., model_width:]
    init_top = jnp.full((rows_here, H, tokens_here), masked_value, jnp.float32)
    init_mass = jnp.zeros((rows_here, H, tokens_here), jnp.float32)
    stats_fold = stats_update(query_heads, query_pos, doc_ids)
    running_top, row_mass = stats_fold(
        (init_top, init_mass),
        (
            lax.all_gather(key_values[..., :model_width], "seq", axis=1, tiled=True),
            lax.all_gather(doc_ids, "seq", axis=1, tiled=True),
        ),
        jnp.int32(0),
    )
    out_fold = output_update(query_heads, query_pos, doc_ids, running_top, row_mass)
    zero_rows = jnp.zeros((rows_here, tokens_here, model_width), jnp.float32)
    attended = out_fold(
        zero_rows,
        (
            lax.all_gather(key_values, "seq", axis=1, tiled=True),
            lax.all_gather(doc_ids, "seq", axis=1, tiled=True),
        ),
        jnp.int32(0),
    )
    attended_low = attended.astype(jnp.bfloat16)
    branch_one = matmul_rows(attended_low, out_weight) + out_bias
    middle = residual + branch_scale * branch_one
    normed_second, second_pull = jax.vjp(layer_norm, middle, second_gain, second_shift)
    normed_second_low = normed_second.astype(jnp.bfloat16)
    hidden = matmul_rows(normed_second_low, fc_weight) + fc_bias
    activated, gelu_pull = jax.vjp(gelu_tanh, hidden)
    activated_low = activated.astype(jnp.bfloat16)
    branch_two = matmul_rows(activated_low, proj_weight) + proj_bias
    output = (middle + branch_scale * branch_two).astype(jnp.bfloat16)
    grad_output = cotangent.astype(jnp.float32)
    grad_branch_two = (branch_scale * grad_output).astype(jnp.bfloat16)
    grad_proj_weight = weight_grad(activated_low, grad_branch_two)
    grad_proj_bias = column_sums(grad_branch_two)
    grad_activated = back_rows(grad_branch_two, proj_weight)
    grad_hidden = gelu_pull(grad_activated)[0].astype(jnp.bfloat16)
    grad_fc_weight = weight_grad(normed_second_low, grad_hidden)
    grad_fc_bias = column_sums(grad_hidden)
    grad_normed_second = back_rows(grad_hidden, fc_weight)
    grad_from_norm, grad_second_gain, grad_second_shift = second_pull(grad_normed_second)
    grad_middle = grad_output + grad_from_norm
    grad_branch_one = (branch_scale * grad_middle).astype(jnp.bfloat16)
    grad_out_weight = weight_grad(attended_low, grad_branch_one)
    grad_out_bias = column_sums(grad_branch_one)
    grad_attended = back_rows(grad_branch_one, out_weight).astype(jnp.bfloat16)
    grad_heads = grad_attended.reshape(rows_here, tokens_here, H, HD)
    row_delta = jnp.einsum(
        "rqhd,rqhd->rhq",
        grad_heads.astype(jnp.float32),
        attended.reshape(rows_here, tokens_here, H, HD),
    )
    back_fold = backward_update(
        query_heads, grad_heads, query_pos, doc_ids, running_top, row_mass, row_delta
    )
    back_initial = (
        jnp.zeros((rows_here, tokens_here, model_width), jnp.float32),
        jnp.zeros((rows_here, tokens_here * seq_count, 2 * model_width), jnp.float32),
    )
    grad_query, kv_grads = back_fold(
        back_initial,
        (
            lax.all_gather(key_values, "seq", axis=1, tiled=True),
            lax.all_gather(doc_ids, "seq", axis=1, tiled=True),
        ),
        jnp.int32(0),
    )
    kv_summed = lax.psum_scatter(
        kv_grads.astype(jnp.bfloat16), "seq", scatter_dimension=1, tiled=True
    )
    grad_mixed = jnp.concatenate([grad_query.astype(jnp.bfloat16), kv_summed], axis=-1)
    grad_qkv_weight = weight_grad(normed_first_low, grad_mixed)
    mixed_sums = column_sums(grad_mixed)
    grad_query_bias = mixed_sums[:model_width]
    grad_value_bias = mixed_sums[2 * model_width :]
    grad_normed_first = back_rows(grad_mixed, qkv_weight)
    grad_from_first, grad_first_gain, grad_first_shift = first_pull(grad_normed_first)
    grad_inputs = (grad_middle + grad_from_first).astype(jnp.bfloat16)
    all_shares = (
        lax.psum_scatter(
            grad_first_gain.astype(jnp.bfloat16), "rows", scatter_dimension=0, tiled=True
        ).astype(jnp.float32),
        lax.psum_scatter(
            grad_first_shift.astype(jnp.bfloat16), "rows", scatter_dimension=0, tiled=True
        ).astype(jnp.float32),
        lax.psum_scatter(
            grad_qkv_weight.astype(jnp.bfloat16), "rows", scatter_dimension=0, tiled=True
        ).astype(jnp.float32),
        lax.psum_scatter(
            grad_query_bias.astype(jnp.bfloat16), "rows", scatter_dimension=0, tiled=True
        ).astype(jnp.float32),
        lax.psum_scatter(
            grad_value_bias.astype(jnp.bfloat16), "rows", scatter_dimension=0, tiled=True
        ).astype(jnp.float32),
        lax.psum_scatter(
            grad_out_weight.astype(jnp.bfloat16), "rows", scatter_dimension=0, tiled=True
        ).astype(jnp.float32),
        lax.psum_scatter(
            grad_out_bias.astype(jnp.bfloat16), "rows", scatter_dimension=0, tiled=True
        ).astype(jnp.float32),
        lax.psum_scatter(
            grad_second_gain.astype(jnp.bfloat16), "rows", scatter_dimension=0, tiled=True
        ).astype(jnp.float32),
        lax.psum_scatter(
            grad_second_shift.astype(jnp.bfloat16), "rows", scatter_dimension=0, tiled=True
        ).astype(jnp.float32),
        lax.psum_scatter(
            grad_fc_weight.astype(jnp.bfloat16), "rows", scatter_dimension=0, tiled=True
        ).astype(jnp.float32),
        lax.psum_scatter(
            grad_fc_bias.astype(jnp.bfloat16), "rows", scatter_dimension=0, tiled=True
        ).astype(jnp.float32),
        lax.psum_scatter(
            grad_proj_weight.astype(jnp.bfloat16), "rows", scatter_dimension=0, tiled=True
        ).astype(jnp.float32),
        lax.psum_scatter(
            grad_proj_bias.astype(jnp.bfloat16), "rows", scatter_dimension=0, tiled=True
        ).astype(jnp.float32),
    )
    (
        grad_first_gain,
        grad_first_shift,
        grad_qkv_weight,
        grad_query_bias,
        grad_value_bias,
        grad_out_weight,
        grad_out_bias,
        grad_second_gain,
        grad_second_shift,
        grad_fc_weight,
        grad_fc_bias,
        grad_proj_weight,
        grad_proj_bias,
    ) = (
        lax.psum(all_shares[0].astype(jnp.bfloat16), "seq").astype(jnp.float32),
        lax.psum(all_shares[1].astype(jnp.bfloat16), "seq").astype(jnp.float32),
        lax.psum(all_shares[2].astype(jnp.bfloat16), "seq").astype(jnp.float32),
        lax.psum(all_shares[3].astype(jnp.bfloat16), "seq").astype(jnp.float32),
        lax.psum(all_shares[4].astype(jnp.bfloat16), "seq").astype(jnp.float32),
        lax.psum(all_shares[5].astype(jnp.bfloat16), "seq").astype(jnp.float32),
        lax.psum(all_shares[6].astype(jnp.bfloat16), "seq").astype(jnp.float32),
        lax.psum(all_shares[7].astype(jnp.bfloat16), "seq").astype(jnp.float32),
        lax.psum(all_shares[8].astype(jnp.bfloat16), "seq").astype(jnp.float32),
        lax.psum(all_shares[9].astype(jnp.bfloat16), "seq").astype(jnp.float32),
        lax.psum(all_shares[10].astype(jnp.bfloat16), "seq").astype(jnp.float32),
        lax.psum(all_shares[11].astype(jnp.bfloat16), "seq").astype(jnp.float32),
        lax.psum(all_shares[12].astype(jnp.bfloat16), "seq").astype(jnp.float32),
    )
    return (
        output,
        grad_inputs,
        grad_first_gain,
        grad_first_shift,
        grad_qkv_weight,
        grad_query_bias,
        grad_value_bias,
        grad_out_weight,
        grad_out_bias,
        grad_second_gain,
        grad_second_shift,
        grad_fc_weight,
        grad_fc_bias,
        grad_proj_weight,
        grad_proj_bias,
    )


def local_rows(
    inputs,
    doc_ids,
    first_gain,
    first_shift,
    qkv_weight,
    query_bias,
    value_bias,
    out_weight,
    out_bias,
    second_gain,
    second_shift,
    fc_weight,
    fc_bias,
    proj_weight,
    proj_bias,
    cotangent,
):
    row_docs = swap_in(doc_ids)
    doc_row, doc_col = row_docs[None, :], row_docs[:, None]
    inputs_row = swap_in(inputs)
    normed_first_low = layer_norm(inputs_row.astype(F32), first_gain, first_shift).astype(BF)
    bias_row = jnp.concatenate([query_bias, jnp.zeros_like(query_bias), value_bias])
    mixed = (jnp.dot(normed_first_low, qkv_weight, preferred_element_type=F32) + bias_row).astype(BF)
    cot_row = swap_in(cotangent)
    attended_low, lse = attend(mixed, doc_row, doc_col)
    zero = jnp.zeros_like(out_bias)
    vec_in = jnp.stack([out_bias, second_gain, second_shift, proj_bias, first_gain, first_shift, zero, zero])
    output, grad_inputs, share_f, share_p, vecs = back(
        "rc", inputs_row, attended_low, cot_row, mixed, lse, doc_row, doc_col, out_weight, fc_weight, proj_weight, qkv_weight, vec_in, fc_bias[None]
    )
    place = lax.axis_index("rows")
    count = NB
    mine = lax.dynamic_slice_in_dim(vecs[:8], place * count, count, 1)
    fc_bias_share = lax.dynamic_slice_in_dim(vecs[8:12].reshape(-1), place * 4 * count, 4 * count, 0)
    fc_share = jnp.concatenate([share_f[u] for u in range(4)], axis=1)
    qkv_share = jnp.concatenate(
        [share_f[5 + m][:, part * 256 : (part + 1) * 256] for part in range(3) for m in range(3)], axis=1
    )
    return (
        output,
        grad_inputs,
        mine[4],
        mine[5],
        qkv_share,
        mine[6],
        mine[7],
        share_f[4],
        mine[2],
        mine[0],
        mine[1],
        fc_share,
        fc_bias_share,
        share_p.reshape(4 * count, -1),
        mine[3],
    )


def solution(mesh):
    in_specs = (
        P("rows", "seq", None),
        P("rows", "seq"),
        P(),
        P(),
        P(),
        P(),
        P(),
        P(),
        P(),
        P(),
        P(),
        P(),
        P(),
        P(),
        P(),
        P("rows", "seq", None),
    )
    out_specs = (
        P("rows", "seq", None),
        P("rows", "seq", None),
        P("rows"),
        P("rows"),
        P("rows", None),
        P("rows"),
        P("rows"),
        P("rows", None),
        P("rows"),
        P("rows"),
        P("rows"),
        P("rows", None),
        P("rows"),
        P("rows", None),
        P("rows"),
    )
    sizes = dict(mesh.shape)

    def chosen(inputs, *others):
        whole_rows = sizes["seq"] == 2 and sizes["rows"] == 16 and inputs.shape[0] == 2
        return (local_rows if whole_rows else local)(inputs, *others)

    return jax.shard_map(chosen, mesh=mesh, in_specs=in_specs, out_specs=out_specs, check_vma=False)
```

```python
import functools
import math

import jax
import jax.numpy as jnp
from jax import lax
from jax.experimental import pallas as pl
from jax.experimental.pallas import tpu as pltpu
from jax.sharding import PartitionSpec as P

H = 12
HD = 64
LAYERS = 12


epsilon = 1e-05
masked_value = -1e30


def layer_norm(values, norm_gain, norm_bias):
    row_mean = jnp.mean(values, axis=-1, keepdims=True)
    centred = values - row_mean
    variance = jnp.mean(centred * centred, axis=-1, keepdims=True)
    return centred * lax.rsqrt(variance + epsilon) * norm_gain + norm_bias


def gelu_tanh(values):
    return jax.nn.gelu(values, approximate=True)


def matmul_rows(left_side, weight):
    flat_rows = left_side.reshape(-1, left_side.shape[-1])
    result = jnp.dot(flat_rows, weight, preferred_element_type=jnp.float32)
    return result.reshape(left_side.shape[:-1] + (weight.shape[1],))


def back_rows(grads_low, weight):
    flat_rows = grads_low.reshape(-1, grads_low.shape[-1])
    result = jnp.einsum("nm,km->nk", flat_rows, weight, preferred_element_type=jnp.float32)
    return result.reshape(grads_low.shape[:-1] + (weight.shape[0],))


def weight_grad(left_side, right_side):
    left_flat = left_side.reshape(-1, left_side.shape[-1])
    right_flat = right_side.reshape(-1, right_side.shape[-1])
    return jnp.einsum("nk,nm->km", left_flat, right_flat, preferred_element_type=jnp.float32)


def column_sums(values):
    return jnp.sum(values.astype(jnp.float32), axis=(0, 1))


def visible(query_pos, query_doc, key_pos, key_doc):
    causal = key_pos[None, None, :] <= query_pos[None, :, None]
    same_doc = key_doc[:, None, :] == query_doc[:, :, None]
    return (causal & same_doc)[:, None]


def split_heads(kv_part):
    rows_here, key_count = (kv_part.shape[0], kv_part.shape[1])
    model_width = H * HD
    key_heads = kv_part[..., :model_width].reshape(rows_here, key_count, H, HD)
    return (key_heads, rows_here, key_count)


def scaled_scores(query_heads, key_heads, allowed):
    raw_scores = jnp.einsum(
        "rqhd,rkhd->rhqk", query_heads, key_heads, preferred_element_type=jnp.float32
    )
    return jnp.where(allowed, raw_scores * HD ** (-0.5), masked_value)


def guarded(folder, query_pos, query_doc):

    def update(totals, portion, offset):
        doc_part = portion[1]
        early_enough = offset <= query_pos[-1]
        doc_meets = jnp.any(jnp.max(doc_part, axis=1) >= jnp.min(query_doc, axis=1))
        return lax.cond(
            early_enough & doc_meets,
            lambda carried: folder(carried, portion, offset),
            lambda carried: carried,
            totals,
        )

    return update


def stats_update(query_heads, query_pos, query_doc):

    def update(totals, portion, offset):
        running_top, row_mass = totals
        kv_part, doc_part = portion
        key_heads, rows_here, key_count = split_heads(kv_part)
        key_pos = jnp.arange(key_count, dtype=jnp.int32)
        allowed = visible(query_pos, query_doc, key_pos, doc_part)
        scores = scaled_scores(query_heads, key_heads, allowed)
        new_top = jnp.maximum(running_top, jnp.max(scores, axis=-1))
        weights = jnp.where(allowed, jnp.exp(scores - new_top[..., None]), 0.0)
        row_mass = jnp.sum(weights, axis=-1)
        return (new_top, row_mass)

    return guarded(update, query_pos, query_doc)


def output_update(query_heads, query_pos, query_doc, running_top, row_mass):

    def update(totals, portion, offset):
        kv_part, doc_part = portion
        key_heads, rows_here, key_count = split_heads(kv_part)
        value_heads = kv_part[..., H * HD :].reshape(rows_here, key_count, H, HD)
        key_pos = jnp.arange(key_count, dtype=jnp.int32)
        allowed = visible(query_pos, query_doc, key_pos, doc_part)
        scores = scaled_scores(query_heads, key_heads, allowed)
        attn_probs = (
            jnp.where(allowed, jnp.exp(scores - running_top[..., None]), 0.0) / row_mass[..., None]
        )
        result = jnp.einsum(
            "rhqk,rkhd->rqhd",
            attn_probs.astype(jnp.bfloat16),
            value_heads,
            preferred_element_type=jnp.float32,
        )
        return result.reshape(totals.shape)

    return guarded(update, query_pos, query_doc)


def backward_update(
    query_heads, grad_heads, query_pos, query_doc, running_top, row_mass, row_delta
):

    def update(totals, portion, offset):
        grad_query, kv_grads = totals
        kv_part, doc_part = portion
        key_heads, rows_here, key_count = split_heads(kv_part)
        value_heads = kv_part[..., H * HD :].reshape(rows_here, key_count, H, HD)
        key_pos = jnp.arange(key_count, dtype=jnp.int32)
        allowed = visible(query_pos, query_doc, key_pos, doc_part)
        scores = scaled_scores(query_heads, key_heads, allowed)
        attn_probs = (
            jnp.where(allowed, jnp.exp(scores - running_top[..., None]), 0.0) / row_mass[..., None]
        )
        grad_probs = jnp.einsum(
            "rqhd,rkhd->rhqk", grad_heads, value_heads, preferred_element_type=jnp.float32
        )
        grad_scores = (attn_probs * (grad_probs - row_delta[..., None]) * HD ** (-0.5)).astype(
            jnp.bfloat16
        )
        query_part = jnp.einsum(
            "rhqk,rkhd->rqhd", grad_scores, key_heads, preferred_element_type=jnp.float32
        )
        grad_query = query_part.reshape(grad_query.shape)
        key_part = jnp.einsum(
            "rhqk,rqhd->rkhd", grad_scores, query_heads, preferred_element_type=jnp.float32
        )
        value_part = jnp.einsum(
            "rhqk,rqhd->rkhd",
            attn_probs.astype(jnp.bfloat16),
            grad_heads,
            preferred_element_type=jnp.float32,
        )
        piece_grads = jnp.concatenate(
            [
                key_part.reshape(rows_here, key_count, H * HD),
                value_part.reshape(rows_here, key_count, H * HD),
            ],
            axis=-1,
        )
        kv_grads = piece_grads
        return (grad_query, kv_grads)

    return guarded(update, query_pos, query_doc)


BF=jnp.bfloat16; F32=jnp.float32
NT=(((1,),(1,)),((),()))
NN=(((1,),(0,)),((),()))
C2=0.125*math.log2(math.e)
QB=256
def dot(a,b,dn=NN): return lax.dot_general(a,b,dn,preferred_element_type=F32)
def half_mask(x,h):
    lane=lax.broadcasted_iota(jnp.int32,x.shape,1)
    return jnp.where((lane<64) if h==0 else (lane>=64), x, jnp.zeros_like(x))
TN=(((0,),(0,)),((),()))
D=768
SC=12**-0.5
EPS=1e-5
G0=math.sqrt(2/math.pi); G1=0.044715
TB=256
def ln_stats(x):
    mean=jnp.mean(x,axis=-1,keepdims=True); c=x-mean
    var=jnp.mean(c*c,axis=-1,keepdims=True)
    r=lax.rsqrt(var+EPS)
    return c*r, r
def step_first(x_ref,att_ref,cot_ref,outw_ref,outb,gain,shift,mid,n2,gb2,b2,e):
    T=mid.shape[0]
    for t in range(0,T,TB):
        sl=slice(t,t+TB)
        m=x_ref[sl].astype(F32)+(dot(att_ref[sl],outw_ref[...])+outb[...])*SC
        mid[sl]=m
        xh,_=ln_stats(m)
        n2[sl]=(xh*gain[...]+shift[...]).astype(BF)
        gb2[sl]=(cot_ref[sl].astype(F32)*SC).astype(BF)
        b2[sl]=jnp.zeros((TB,D),F32); e[sl]=jnp.zeros((TB,D),F32)
def gelu_both(h):
    h2=h*h
    t=jnp.tanh(h*(G0+(G0*G1)*h2))
    half=0.5*(1+t)
    act=h*half
    dg=half+act*(1-t)*(G0+(3*G0*G1)*h2)
    return act,dg
def step_ff(fcw,fcb,projw,n2,gb2,acts,dhs,b2,e,gfc,gproj,gfcb,hook):
    T=n2.shape[0]
    cs=jnp.zeros((1,fcw.shape[1]),F32)
    blocks=[slice(t,t+TB) for t in range(0,T,TB)]
    first=lambda sl:(dot(n2[sl],fcw[...])+fcb[...], dot(gb2[sl],projw[...],NT))
    now=first(blocks[0])
    hook(0)
    for k,sl in enumerate(blocks):
        later=first(blocks[k+1]) if k+1<len(blocks) else None
        h,dA=now
        act,dg=gelu_both(h)
        ab=act.astype(BF); acts[sl]=ab
        dh=(dA*dg).astype(BF); dhs[sl]=dh
        cs=cs+jnp.sum(dh.astype(F32),axis=0,keepdims=True)
        b2[sl]+=dot(ab,projw[...])
        e[sl]+=dot(dh,fcw[...],NT)
        now=later
        hook(k+1)
    gfcb[...]=cs
    gproj(dot(acts[...],gb2[...],TN).astype(BF))
    hook(5)
    gfc(dot(n2[...],dhs[...],TN).astype(BF))
    hook(6)
def step_after(cot_ref,att_ref,outw_ref,projb,gain,mid,b2,e,gb2,out,gb1,do,gout,vecs,after_out):
    T=mid.shape[0]
    for t in range(0,T,TB):
        sl=slice(t,t+TB)
        out[sl]=(mid[sl]+(b2[sl]+projb[...])*SC).astype(BF)
    after_out()
    z=jnp.zeros((1,D),F32); sg=z; ss=z; sb1=z; sb2=z
    for t in range(0,T,TB):
        sl=slice(t,t+TB)
        m=mid[sl]
        xh,r=ln_stats(m)
        ee=e[sl]
        sg=sg+jnp.sum(ee*xh,axis=0,keepdims=True); ss=ss+jnp.sum(ee,axis=0,keepdims=True)
        g=ee*gain[...]
        gm=cot_ref[sl].astype(F32)+r*(g-jnp.mean(g,axis=-1,keepdims=True)-xh*jnp.mean(g*xh,axis=-1,keepdims=True))
        mid[sl]=gm
        b1=(gm*SC).astype(BF); gb1[sl]=b1
        sb1=sb1+jnp.sum(b1.astype(F32),axis=0,keepdims=True); sb2=sb2+jnp.sum(gb2[sl].astype(F32),axis=0,keepdims=True)
        do[sl]=dot(b1,outw_ref[...],NT).astype(BF)
    gout(dot(att_ref[...],gb1[...],TN).astype(BF))
    for k,v in enumerate((sg,ss,sb1,sb2)): vecs[k:k+1,:]=v
MESH=pl.DeviceIdType.MESH
CH=128
def first_seen(docs):
    T=docs.shape[1]
    place=lax.broadcasted_iota(jnp.int32,docs.shape,1)
    before=pltpu.roll(docs,1,1)
    start=jnp.where((docs!=before)&(place>0),place,0)
    sh=1
    while sh<T:
        start=jnp.maximum(start,jnp.where(place>=sh,pltpu.roll(start,sh,1),0))
        sh*=2
    return start
def build_bias_tri(start,bias,T):
    for i in range(T//QB):
        kk=(i+1)*QB; b0=i*(i+1)//2*QB
        key=lax.broadcasted_iota(jnp.int32,(kk,QB),0); qry=lax.broadcasted_iota(jnp.int32,(kk,QB),1)+i*QB
        ok=(key<=qry)&(key>=start[:,i*QB:kk])
        bias[b0:b0+kk,:]=jnp.where(ok,0.0,-1e30)
def front_kernel(inp,cot,docs,v0,v1,v2,v3,v4,v5,v6,v7,qkvw,xrow,cotrow,mixed,att,lse_ref,start_ref,vec_in,xs,wv,mx,dr,bias,oT,send,recv,loc,wsem,osem):
    step=pl.program_id(0)
    T=mx.shape[0]; half=T//2; n=half//CH
    s=lax.axis_index("seq"); r=lax.axis_index("rows")
    peer=(1-s,r)
    row=lambda k: vec_in[k:k+1,:]
    def remote(src,dst,k): return pltpu.make_async_remote_copy(src_ref=src,dst_ref=dst,send_sem=send.at[k],recv_sem=recv.at[k],device_id=peer,device_id_type=MESH)
    def x_copy(c): return remote(inp.at[1-s,pl.ds(c*CH,CH)],xs.at[s,pl.ds(c*CH,CH)],c)
    def d_copy(): return remote(docs.at[pl.ds(1-s,1)],dr.at[pl.ds(s,1)],n)
    def cot_copy(): return remote(cot.at[1-s],cotrow.at[s],n+1)
    def own(k):
        one=pl.ds(s,1)
        src,dst=((inp.at[s],xs.at[s]),(docs.at[one],dr.at[one]),(cot.at[s],cotrow.at[s]))[k]
        return pltpu.make_async_copy(src,dst,loc.at[k])
    def rows_out(h): return pltpu.make_async_copy(xs.at[h],xrow.at[h],osem.at[h])
    def mixed_out(h): return pltpu.make_async_copy(mx.at[pl.ds(h*half,half)],mixed.at[pl.ds(h*half,half)],osem.at[2+h])
    def project(h,t,size):
        xh,_=ln_stats(xs[h,pl.ds(t,size)].astype(F32))
        nb=(xh*row(4)+row(5)).astype(BF)
        at=pl.ds(pl.multiple_of(h*half+t,CH),size)
        mx[at,0:D]=(dot(nb,wv[:,0:D])+row(6)).astype(BF)
        mx[at,D:2*D]=dot(nb,wv[:,D:2*D]).astype(BF)
        mx[at,2*D:3*D]=(dot(nb,wv[:,2*D:3*D])+row(7)).astype(BF)
    @pl.when(step==0)
    def _():
        bar=pltpu.get_barrier_semaphore()
        pl.semaphore_signal(bar,inc=1,device_id=peer,device_id_type=MESH)
        own(0).start(); own(1).start()
        for k,v in enumerate((v0,v1,v2,v3,v4,v5,v6,v7)): vec_in[k:k+1,:]=v[...].reshape(1,D)
        weight=pltpu.make_async_copy(qkvw,wv,wsem)
        weight.start()
        pl.semaphore_wait(bar,1)
        d_copy().start()
        for c in range(n): x_copy(c).start()
        cot_copy().start()
        own(2).start()
        own(0).wait(); weight.wait()
        for t in range(0,half,TB): project(s,t,TB)
        own(1).wait(); d_copy().wait_recv()
        docs_row=jnp.concatenate([dr[0:1,:],dr[1:2,:]],axis=1)
        start=first_seen(docs_row)
        start_ref[...]=start
        build_bias_tri(start,bias,T)
        for c in range(n):
            x_copy(c).wait_recv()
            project(1-s,c*CH,CH)
        for h in range(2): rows_out(h).start(); mixed_out(h).start()
    @pl.when(step>0)
    def _():
        p=step-1
        cols=lambda base: pl.ds(pl.multiple_of(base+p*128,128),128)
        q=mx[:,cols(0)]; k=mx[:,cols(D)]
        vT=mx[:,cols(2*D)].astype(F32).T.astype(BF)
        queries=[half_mask(q,h) for h in range(2)]
        def scores(h,i):
            kk=(i+1)*QB; b0=i*(i+1)//2*QB
            return dot(k[:kk],queries[h][i*QB:kk],NT)*C2+bias[b0:b0+kk,:]
        jobs=[(h,i) for i in range(T//QB) for h in range(2)]
        res={}
        now=scores(*jobs[0])
        for a,(h,i) in enumerate(jobs):
            later=scores(*jobs[a+1]) if a+1<len(jobs) else None
            kk=(i+1)*QB
            top=jnp.max(now,axis=0,keepdims=True)
            probs=jnp.exp2(now-top)
            mass=jnp.sum(probs,axis=0,keepdims=True)
            part=dot(vT[h*64:(h+1)*64,:kk],probs.astype(BF))
            res[h,i]=(part/mass,top+jnp.log2(mass))
            now=later
        for (h,i),(part,lse) in res.items():
            sl=slice(i*QB,(i+1)*QB)
            oT[h*64:(h+1)*64,sl]=part; lse_ref[0,h:h+1,sl]=lse
        att[...]=oT[...].T.astype(BF)
    @pl.when(step==6)
    def _():
        for h in range(2): rows_out(h).wait(); mixed_out(h).wait()
        for c in range(n): x_copy(c).wait_send()
        d_copy().wait_send()
        cot_copy().wait(); own(2).wait()
def front(inp,cot,docs,vectors,qkvw):
    T=2*inp.shape[1]; half=T//2
    S=jax.ShapeDtypeStruct; V=pltpu.VMEM
    anyw=pl.BlockSpec(memory_space=pl.ANY)
    pos=lambda s: jnp.maximum(s-1,0)
    n=half//CH
    DMA=pltpu.SemaphoreType.DMA
    return pl.pallas_call(front_kernel,grid=(7,),
      in_specs=[anyw,anyw,anyw]+[pl.BlockSpec((D,),lambda s:(0,))]*8+[anyw],
      out_shape=(S((2,half,D),BF),S((2,half,D),BF),S((T,3*D),BF),S((T,D),BF),S((6,2,T),F32),S((1,T),jnp.int32),S((8,D),F32)),
      out_specs=(anyw,anyw,anyw,pl.BlockSpec((T,128),lambda s:(0,pos(s))),pl.BlockSpec((1,2,T),lambda s:(pos(s),0,0)),pl.BlockSpec((1,T),lambda s:(0,0)),pl.BlockSpec((8,D),lambda s:(0,0))),
      scratch_shapes=[V((2,half,D),BF),V((D,3*D),BF),V((T,3*D),BF),V((2,half),jnp.int32),V((10*QB,QB),F32),V((128,T),F32),
        DMA((n+2,)),DMA((n+2,)),DMA((3,)),DMA,DMA((4,))],
      compiler_params=pltpu.CompilerParams(vmem_limit_bytes=64<<20,collective_id=2,has_side_effects=True,dimension_semantics=("arbitrary",)),name="front")(inp,cot,docs,*vectors,qkvw)
NB=48
ZFIRST=(0,1,2,3)
def add_low(a,b): return (a.astype(F32)+b.astype(F32)).astype(BF)
class Sums:
    def __init__(self,refs,sems,outs):
        (self.gf,self.gp,self.rf,self.rp,self.a,self.ap,self.b1,self.b1p,self.b2,self.b2p,self.b3,self.b3p,self.b4,self.b4p,self.vs,self.vr)=refs
        (self.cs,self.cr,self.credit,s1,r1,s2,r2,s3,r3,s4,r4,self.vss,self.vsr)=sems
        self.sem=((s1,r1),(s2,r2),(s3,r3),(s4,r4))
        self.out_qkv,self.out_ow,self.out_fc,self.out_proj=outs
        self.s=lax.axis_index("seq"); r=lax.axis_index("rows"); self.r=r
        self.core=lax.rem(r,2); self.x=lax.rem(r//2,2); self.zl=lax.rem(r//4,2); self.zh=r//8
        flip=lambda d,bit:(self.s, r+d-2*d*bit)
        self.peer=dict(c=flip(1,self.core),x=flip(2,self.x),z1=flip(4,self.zl),z2=flip(8,self.zh),y=(1-self.s,r))
    def greet(self):
        bar=pltpu.get_barrier_semaphore()
        for d in self.peer.values(): pl.semaphore_signal(bar,inc=1,device_id=d,device_id_type=MESH)
    def meet(self):
        pl.semaphore_wait(pltpu.get_barrier_semaphore(),len(self.peer))
    def copy(self,src,dst,ss,rs,to):
        return pltpu.make_async_remote_copy(src_ref=src,dst_ref=dst,send_sem=ss,recv_sem=rs,device_id=self.peer[to],device_id_type=MESH)
    def c_copy(self,kind):
        if kind=="f": return [self.copy(self.gf.at[:,1-self.core],self.rf,self.cs.at[0],self.cr.at[0],"c")]
        return [self.copy(self.gp.at[x,1-self.core],self.rp.at[:,x],self.cs.at[1+x],self.cr.at[1+x],"c") for x in range(2)]
    def c_start(self,kind,first):
        k=0 if kind=="f" else 1
        @pl.when(jnp.logical_not(first))
        def _(): pl.semaphore_wait(self.credit.at[k],1)
        for c in self.c_copy(kind): c.start()
    def c_finish(self,kind,u):
        for c in self.c_copy(kind): c.wait()
        if kind=="f":
            for i in range(8):
                self.a[u,i//4,(i//2)%2,i%2]=add_low(self.gf[i,self.core],self.rf[i])
        else:
            for t in range(4):
                for x in range(2):
                    self.ap[u//2,u%2,t,x]=add_low(self.gp[x,self.core,t],self.rp[t,x])
        if u<(7 if kind=="f" else 3):
            pl.semaphore_signal(self.credit.at[0 if kind=="f" else 1],inc=1,device_id=self.peer["c"],device_id_type=MESH)
    def part(self,kind,u,stage):
        x,zh,zl=self.x,self.zh,self.zl
        if kind=="f":
            a=self.a
            land=(self.b1,self.b2,self.b3,self.b4)[stage-1].at[u]
            if stage==4: return a.at[u,zh,zl,x],land,"y",[((u,zh,zl,x),())]
            if u in ZFIRST:
                if stage==1: return a.at[u,:,1-zl],land,"z1",[((u,i,zl,k),(i,k)) for i in range(2) for k in range(2)]
                if stage==2: return a.at[u,1-zh,zl],land,"z2",[((u,zh,zl,k),(k,)) for k in range(2)]
                return a.at[u,zh,zl,1-x],land,"x",[((u,zh,zl,x),())]
            if stage==1: return a.at[u,:,:,1-x],land,"x",[((u,i,k,x),(i,k)) for i in range(2) for k in range(2)]
            if stage==2: return a.at[u,:,1-zl,x],land,"z1",[((u,i,zl,x),(i,)) for i in range(2)]
            return a.at[u,1-zh,zl,x],land,"z2",[((u,zh,zl,x),())]
        ap=self.ap
        land=(self.b1p,self.b2p,self.b3p,self.b4p)[stage-1].at[u]
        if stage==1: return ap.at[u//2,u%2,:,1-x],land,"x",[((u//2,u%2,t,x),(t,)) for t in range(4)]
        if stage==2: return ap.at[:,1-zl,u,x],land,"z1",[((i,zl,u,x),(i,)) for i in range(2)]
        if stage==3: return ap.at[1-zh,zl,u,x],land,"z2",[((zh,zl,u,x),())]
        return ap.at[zh,zl,u,x],land,"y",[((zh,zl,u,x),())]
    def move(self,kind,u,stage):
        src,dst,to,_=self.part(kind,u,stage)
        k=u if kind=="f" else 8+u
        ss,rs=self.sem[stage-1]
        return self.copy(src,dst,ss.at[k],rs.at[k],to)
    def start(self,kind,u,stage): self.move(kind,u,stage).start()
    def finish(self,kind,u,stage):
        self.move(kind,u,stage).wait_recv()
        _,land,_,pairs=self.part(kind,u,stage)
        own=self.a if kind=="f" else self.ap
        for at,got in pairs:
            if stage<4: own[at]=add_low(own[at],land[got] if got else land[...])
            else: self.deliver(kind,u,own[at].astype(F32)+land[...].astype(F32))
        if stage<4 and not (kind=="p" and stage==1): self.start(kind,u,stage+1)
    def deliver(self,kind,u,total):
        if kind=="p": self.out_proj[u*NB:(u+1)*NB,:]=total
        elif u<4: self.out_fc[:,u*D:(u+1)*D]=total
        elif u==4: self.out_ow[...]=total
        else:
            for part in range(3):
                at=part*D+(u-5)*256
                self.out_qkv[:,at:at+256]=total[:,part*256:(part+1)*256]
    def wait_sends(self,kind,u):
        for stage in (1,2,3,4): self.move(kind,u,stage).wait_send()
    def v_copy(self,k):
        return self.copy(self.vs.at[k],self.vr.at[k],self.vss.at[k],self.vsr.at[k],("c","x","z1","z2","y")[k])
    def v_finish(self,k):
        self.v_copy(k).wait()
        self.vs[k+1]=self.vs[k]+self.vr[k]
        if k<4: self.v_copy(k+1).start()

def attn_pair(q_ref,k_ref,v_ref,do,o,lse_ref,bias,dqT,dk,dv,put,hook):
    T=q_ref.shape[0]
    hook(0)
    prod=(do.astype(F32)*o.astype(F32)).T
    kT=k_ref[...].astype(F32).T.astype(BF)
    dk[...]=jnp.zeros_like(dk); dv[...]=jnp.zeros_like(dv)
    for h in range(2):
        qh=half_mask(q_ref[...],h); doh=half_mask(do,h)
        delta=jnp.sum(prod[h*64:(h+1)*64],axis=0,keepdims=True)
        for i in range(T//QB):
            kk=(i+1)*QB; sl=slice(i*QB,kk); b0=i*(i+1)//2*QB
            s=dot(k_ref[0:kk,:],qh[sl],NT)*C2+bias[b0:b0+kk,:]
            p=jnp.exp2(s-lse_ref[0,h:h+1,sl])
            dp=dot(v_ref[0:kk,:],doh[sl],NT)
            ds=(p*(dp-delta[:,sl])).astype(BF)
            dv[0:kk,:]+=dot(p.astype(BF),doh[sl])
            dk[0:kk,:]+=dot(ds,qh[sl])
            dqT[h*64:(h+1)*64,sl]=dot(kT[h*64:(h+1)*64,:kk],ds)
        hook(h+1)
    put(0,(dqT[...].T*0.125).astype(BF))
    put(1,(dk[...]*0.125).astype(BF))
    put(2,dv[...].astype(BF))
NSTEP=12
PLAN={}
def plan(text):
    PLAN.clear()
    for line in text.strip().splitlines():
        where,what=line.split(":")
        k,q=where.split(".")
        PLAN.setdefault((int(k),int(q)),[]).extend(what.split())
plan("""
0.5: cs_p0
0.6: cs_f0
1.1: c_p0  s_p0
1.3: c_f0  s_f0
1.5: cs_p1
1.6: cs_f1
2.1: c_p1  s_p1
2.3: c_f1  s_f1
2.5: cs_p2
2.6: cs_f2  1_p0
3.1: 1_f0  c_p2  s_p2
3.3: c_f2  s_f2
3.5: cs_p3
3.6: cs_f3  1_p1
4.1: c_f3  s_f3  1_f1  c_p3  s_p3  2_f0
4.2: cs_f4
4.3: 1_p2
5.1: 1_f2  c_f4  s_f4
6.1: 2_f1
6.3: cs_f5  1_f3  1_p3  z_p0  z_p1  z_p2  z_p3
7.0: 3_f0
7.1: 2_f2  c_f5  s_f5
8.2: 1_f4
8.3: cs_f6  3_f1  2_f3  4_f0
9.0: 2_p0  3_f2
9.1: c_f6  s_f6
9.2: 2_p1
10.2: 2_p2  1_f5  4_f1
10.3: cs_f7  3_f3  3_p0  4_f2
10.4: 2_p3  c_f7  s_f7
11.0: 3_p1  2_f4
11.3: 1_f6  3_p2  4_f3  2_f5  3_p3  4_p0  v0  3_f4  3_f5  2_f6  1_f7  v1  3_f6  2_f7  v2  3_f7  v3  4_p1  4_p2  4_p3  4_f4  4_f5  4_f6  4_f7  v4
""")
def back_kernel(flags,*refs):
    (x,att,cot,outw,fcw,projw,q_ref,k_ref,v_ref,lse_ref,wq,wk,wv,start,vec_in,fcb,
     out_hbm,gin_hbm,out_qkv,out_ow,out_fc,out_proj,vec_out,
     n2,gb2,acts,dhs,b2,e,mid,bias,dqT,dk,dv,fcbs,vecs,
     *rest)=refs
    nsum=16
    S=Sums(rest[:nsum],rest[nsum:nsum+13],(out_qkv,out_ow,out_fc,out_proj))
    swap_s,swap_r,loc=rest[nsum+13:]
    T=mid.shape[0]; half=T//2
    step=pl.program_id(0)
    row=lambda k: vec_in.at[k:k+1]
    OUTB,G2,S2,PB,G1_,S1_=range(6)
    comm="r" in flags; comp="c" in flags
    place=S.s
    def keep_copy(src,dst,k):
        return pltpu.make_async_copy(src.at[pl.ds(place*half,half)],dst.at[place],loc.at[k])
    def give_copy(src,dst,k):
        return S.copy(src.at[pl.ds((1-place)*half,half)],dst.at[place],swap_s.at[k],swap_r.at[k],"y")
    def do(word):
        if word[0]=="v": return S.v_finish(int(word[1:]))
        name,(kind,u)=word.split("_")[0],word.split("_")[1]
        u=int(u)
        if name=="cs": S.c_start(kind,u==0)
        elif name=="c": S.c_finish(kind,u)
        elif name=="s": S.start(kind,u,1)
        elif name=="z": S.start(kind,u,2)
        else: S.finish(kind,u,int(name))
    def hook_for(steps):
        def hook(q):
            if not comm: return
            for k in steps:
                if (k,q) in PLAN:
                    @pl.when(step==k)
                    def _():
                        for word in PLAN[k,q]: do(word)
        return hook
    gf2=lambda val: S.gf.__setitem__(Ellipsis,val.reshape(8,2,NB,D))
    gp2=lambda val: S.gp.__setitem__(Ellipsis,val.reshape(2,2,4,NB,D))
    @pl.when(step==0)
    def _():
        if comm: S.greet()
        step_first(x,att,cot,outw,row(OUTB),row(G2),row(S2),mid,n2,gb2,b2,e)
        if comm: S.meet()
    @pl.when(step<4)
    def _():
        hook=hook_for(range(4))
        if comp: step_ff(fcw,fcb,projw,n2,gb2,acts,dhs,b2,e,gf2,gp2,fcbs.at[pl.ds(step,1)],hook)
        else:
            for q in range(7): hook(q)
    @pl.when(step==4)
    def _():
        hook=hook_for([4])
        hook(0)
        def after_out():
            if comm:
                keep_copy(dhs,out_hbm,0).start(); give_copy(dhs,out_hbm,0).start()
            hook(1)
        if comp:
            step_after(cot,att,outw,row(PB),row(G2),mid,b2,e,gb2,dhs,n2,acts,gf2,vecs,after_out)
        else: after_out()
        hook(2)
        if comp:
            build_bias_tri(start[...],bias,T)
            for t in range(0,T,TB):
                sl=slice(t,t+TB)
                xh,_=ln_stats(x[sl].astype(F32)); gb2[sl]=(xh*row(G1_)[...]+row(S1_)[...]).astype(BF)
                b2[sl]=jnp.zeros((TB,D),F32)
        hook(3)
    @pl.when((step>=5)&(step<11))
    def _():
        p=step-5; par=lax.rem(p,2); m=p//2
        cols=pl.ds(pl.multiple_of(p*128,128),128)
        hook=hook_for(range(5,11))
        def put(part,val):
            n2[:,pl.ds(pl.multiple_of(part*256+par*128,128),128)]=val
            if part!=1:
                vecs[pl.ds(6+part//2,1),cols]=jnp.sum(val.astype(F32),axis=0,keepdims=True)
        if comp: attn_pair(q_ref,k_ref,v_ref,acts[:,cols],att[:,cols],lse_ref,bias,dqT,dk,dv,put,hook)
        else:
            for q in range(3): hook(q)
        @pl.when(par==1)
        def _():
            if comp:
                gf2(dot(gb2[...],n2[...],TN).astype(BF))
            hook(3)
            if comp:
                for t in range(0,T,TB):
                    sl=slice(t,t+TB)
                    b2[sl]+=dot(n2[sl,0:256],wq[...],NT)+dot(n2[sl,256:512],wk[...],NT)+dot(n2[sl,512:768],wv[...],NT)
            hook(4)
    @pl.when(step==11)
    def _():
        hook=hook_for([11])
        if comm:
            keep_copy(dhs,out_hbm,0).wait(); give_copy(dhs,out_hbm,0).wait()
        if comp:
            vecs[4:6,:]=jnp.zeros((2,D),F32)
            def tok(sl):
                xh,r=ln_stats(x[sl].astype(F32)); ee=b2[sl]
                vecs[4:5,:]+=jnp.sum(ee*xh,axis=0,keepdims=True); vecs[5:6,:]+=jnp.sum(ee,axis=0,keepdims=True)
                g=ee*row(G1_)[...]
                dhs[sl]=(mid[sl]+r*(g-jnp.mean(g,axis=-1,keepdims=True)-xh*jnp.mean(g*xh,axis=-1,keepdims=True))).astype(BF)
            for q,part in enumerate((1-place,place)):
                for t in range(0,half,TB):
                    tok(pl.ds(pl.multiple_of(part*half+t,TB),TB))
                if comm: (keep_copy if q else give_copy)(dhs,gin_hbm,1).start()
                hook(q)
        elif comm:
            give_copy(dhs,gin_hbm,1).start(); hook(0); keep_copy(dhs,gin_hbm,1).start(); hook(1)
        if comm:
            S.vs[0,0:8]=vecs[...]; S.vs[0,8:12]=fcbs[...]; S.vs[0,12:16]=jnp.zeros((4,D),F32)
            S.v_copy(0).start()
            hook(2); hook(3)
            vec_out[...]=S.vs[5]
            for u in range(8): S.wait_sends("f",u)
            for u in range(4): S.wait_sends("p",u)
            keep_copy(dhs,gin_hbm,1).wait(); give_copy(dhs,gin_hbm,1).wait()
def back(flags,x,att,cot,mixed,lse,start,outw,fcw,projw,qkvw,vec_in,fcb):
    T=x.shape[0]
    once=pl.Buffered(1)
    full=lambda a,b: pl.BlockSpec((a,b),lambda s:(0,0),pipeline_mode=once)
    j=lambda s: jnp.minimum(s,3)
    p=lambda s: jnp.clip(s-5,0,5)
    m=lambda s: jnp.clip(s-5,0,5)//2
    S=jax.ShapeDtypeStruct
    V=pltpu.VMEM
    return pl.pallas_call(functools.partial(back_kernel,flags),grid=(NSTEP,),
      in_specs=[full(T,D),full(T,D),full(T,D),full(D,D),pl.BlockSpec((D,D),lambda s:(0,j(s))),pl.BlockSpec((D,D),lambda s:(j(s),0)),
        pl.BlockSpec((T,128),lambda s:(0,p(s))),pl.BlockSpec((T,128),lambda s:(0,6+p(s))),pl.BlockSpec((T,128),lambda s:(0,12+p(s))),pl.BlockSpec((1,2,T),lambda s:(p(s),0,0)),
        pl.BlockSpec((D,256),lambda s:(0,m(s))),pl.BlockSpec((D,256),lambda s:(0,3+m(s))),pl.BlockSpec((D,256),lambda s:(0,6+m(s))),
        full(1,T),full(8,D),pl.BlockSpec((1,D),lambda s:(0,j(s)))],
      out_shape=(S((2,T//2,D),BF),S((2,T//2,D),BF),S((NB,3*D),F32),S((NB,D),F32),S((NB,4*D),F32),S((4*NB,D),F32),S((16,D),F32)),
      out_specs=(pl.BlockSpec(memory_space=pl.ANY),pl.BlockSpec(memory_space=pl.ANY),full(NB,3*D),full(NB,D),full(NB,4*D),full(4*NB,D),full(16,D)),
      scratch_shapes=[V((T,D),BF)]*4+[V((T,D),F32)]*3+[V((10*QB,QB),F32),V((128,T),F32),V((T,128),F32),V((T,128),F32),V((4,D),F32),V((8,D),F32)]
        +[V((8,2,NB,D),BF),V((2,2,4,NB,D),BF),V((8,NB,D),BF),V((4,2,NB,D),BF),V((8,2,2,2,NB,D),BF),V((2,2,4,2,NB,D),BF),V((8,2,2,NB,D),BF),V((4,4,NB,D),BF),
          V((8,2,NB,D),BF),V((4,2,NB,D),BF),V((8,NB,D),BF),V((4,NB,D),BF),V((8,NB,D),BF),V((4,NB,D),BF),V((6,16,D),F32),V((5,16,D),F32)]
        +[pltpu.SemaphoreType.DMA((3,)),pltpu.SemaphoreType.DMA((3,)),pltpu.SemaphoreType.REGULAR((2,))]+[pltpu.SemaphoreType.DMA((12,))]*8+[pltpu.SemaphoreType.DMA((5,))]*2
        +[pltpu.SemaphoreType.DMA((2,))]*3,
      compiler_params=pltpu.CompilerParams(vmem_limit_bytes=64<<20,collective_id=1 if "r" in flags else None,has_side_effects=True,dimension_semantics=("arbitrary",)),name="back_"+flags)(x,att,cot,outw,fcw,projw,mixed,mixed,mixed,lse,qkvw,qkvw,qkvw,start,vec_in,fcb)
def tail_kernel(vecs,out_in,gin_in,qkv_in,ow_in,fc_in,proj_in,out,gin,qkv,ow,fc,proj,v0,v1,v2,v3,v4,v5,v6,v7,fcb):
    for a,b in ((out_in,out),(gin_in,gin),(qkv_in,qkv),(ow_in,ow),(fc_in,fc),(proj_in,proj)): b[...]=a[...]
    @pl.when(pl.program_id(0)==0)
    def _():
        r=lax.axis_index("rows")
        turned=pltpu.roll(vecs[0:8,:],lax.rem(16-r,16)*NB,1)
        for k,ref in enumerate((v0,v1,v2,v3,v4,v5,v6,v7)): ref[...]=turned[k:k+1,0:NB]
        line=pltpu.roll(jnp.broadcast_to(vecs[pl.ds(8+r//4,1),:],(8,D)),lax.rem(4-lax.rem(r,4),4)*4*NB,1)
        fcb[...]=line[0:1,0:4*NB]
def tail(vecs,*arrays):
    S=jax.ShapeDtypeStruct
    out,gin,qkv,ow,fc,proj=arrays
    small=[S((1,NB),F32)]*8+[S((1,4*NB),F32)]
    whole=lambda a: pl.BlockSpec(a.shape,lambda g:(0,0))
    halves=[pl.BlockSpec((1,)+out.shape[1:],lambda g:(g,0,0))]*2+[pl.BlockSpec((NB,a.shape[1]//2),lambda g:(0,g)) for a in (qkv,ow,fc)]+[pl.BlockSpec((2*NB,D),lambda g:(g,0))]
    return pl.pallas_call(tail_kernel,grid=(2,),
      in_specs=[whole(vecs)]+halves,
      out_shape=tuple(S(a.shape,a.dtype) for a in arrays)+tuple(small),
      out_specs=tuple(halves)+tuple(whole(a) for a in small),
      compiler_params=pltpu.CompilerParams(vmem_limit_bytes=64<<20,dimension_semantics=("arbitrary",)),
      name="tail")(vecs,*arrays)


def local(
    inputs,
    doc_ids,
    first_gain,
    first_shift,
    qkv_weight,
    query_bias,
    value_bias,
    out_weight,
    out_bias,
    second_gain,
    second_shift,
    fc_weight,
    fc_bias,
    proj_weight,
    proj_bias,
    cotangent,
):
    branch_scale = LAYERS ** (-0.5)
    rows_here, tokens_here, model_width = inputs.shape
    seq_count = lax.axis_size("seq")
    seq_place = lax.axis_index("seq")
    query_pos = seq_place * tokens_here + jnp.arange(tokens_here, dtype=jnp.int32)
    residual = inputs.astype(jnp.float32)
    normed_first, first_pull = jax.vjp(layer_norm, residual, first_gain, first_shift)
    normed_first_low = normed_first.astype(jnp.bfloat16)
    bias_row = jnp.concatenate([query_bias, jnp.zeros_like(query_bias), value_bias])
    mixed_proj = (matmul_rows(normed_first_low, qkv_weight) + bias_row).astype(jnp.bfloat16)
    query_heads = mixed_proj[..., :model_width].reshape(rows_here, tokens_here, H, HD)
    key_values = mixed_proj[..., model_width:]
    init_top = jnp.full((rows_here, H, tokens_here), masked_value, jnp.float32)
    init_mass = jnp.zeros((rows_here, H, tokens_here), jnp.float32)
    stats_fold = stats_update(query_heads, query_pos, doc_ids)
    running_top, row_mass = stats_fold(
        (init_top, init_mass),
        (
            lax.all_gather(key_values[..., :model_width], "seq", axis=1, tiled=True),
            lax.all_gather(doc_ids, "seq", axis=1, tiled=True),
        ),
        jnp.int32(0),
    )
    out_fold = output_update(query_heads, query_pos, doc_ids, running_top, row_mass)
    zero_rows = jnp.zeros((rows_here, tokens_here, model_width), jnp.float32)
    attended = out_fold(
        zero_rows,
        (
            lax.all_gather(key_values, "seq", axis=1, tiled=True),
            lax.all_gather(doc_ids, "seq", axis=1, tiled=True),
        ),
        jnp.int32(0),
    )
    attended_low = attended.astype(jnp.bfloat16)
    branch_one = matmul_rows(attended_low, out_weight) + out_bias
    middle = residual + branch_scale * branch_one
    normed_second, second_pull = jax.vjp(layer_norm, middle, second_gain, second_shift)
    normed_second_low = normed_second.astype(jnp.bfloat16)
    hidden = matmul_rows(normed_second_low, fc_weight) + fc_bias
    activated, gelu_pull = jax.vjp(gelu_tanh, hidden)
    activated_low = activated.astype(jnp.bfloat16)
    branch_two = matmul_rows(activated_low, proj_weight) + proj_bias
    output = (middle + branch_scale * branch_two).astype(jnp.bfloat16)
    grad_output = cotangent.astype(jnp.float32)
    grad_branch_two = (branch_scale * grad_output).astype(jnp.bfloat16)
    grad_proj_weight = weight_grad(activated_low, grad_branch_two)
    grad_proj_bias = column_sums(grad_branch_two)
    grad_activated = back_rows(grad_branch_two, proj_weight)
    grad_hidden = gelu_pull(grad_activated)[0].astype(jnp.bfloat16)
    grad_fc_weight = weight_grad(normed_second_low, grad_hidden)
    grad_fc_bias = column_sums(grad_hidden)
    grad_normed_second = back_rows(grad_hidden, fc_weight)
    grad_from_norm, grad_second_gain, grad_second_shift = second_pull(grad_normed_second)
    grad_middle = grad_output + grad_from_norm
    grad_branch_one = (branch_scale * grad_middle).astype(jnp.bfloat16)
    grad_out_weight = weight_grad(attended_low, grad_branch_one)
    grad_out_bias = column_sums(grad_branch_one)
    grad_attended = back_rows(grad_branch_one, out_weight).astype(jnp.bfloat16)
    grad_heads = grad_attended.reshape(rows_here, tokens_here, H, HD)
    row_delta = jnp.einsum(
        "rqhd,rqhd->rhq",
        grad_heads.astype(jnp.float32),
        attended.reshape(rows_here, tokens_here, H, HD),
    )
    back_fold = backward_update(
        query_heads, grad_heads, query_pos, doc_ids, running_top, row_mass, row_delta
    )
    back_initial = (
        jnp.zeros((rows_here, tokens_here, model_width), jnp.float32),
        jnp.zeros((rows_here, tokens_here * seq_count, 2 * model_width), jnp.float32),
    )
    grad_query, kv_grads = back_fold(
        back_initial,
        (
            lax.all_gather(key_values, "seq", axis=1, tiled=True),
            lax.all_gather(doc_ids, "seq", axis=1, tiled=True),
        ),
        jnp.int32(0),
    )
    kv_summed = lax.psum_scatter(
        kv_grads.astype(jnp.bfloat16), "seq", scatter_dimension=1, tiled=True
    )
    grad_mixed = jnp.concatenate([grad_query.astype(jnp.bfloat16), kv_summed], axis=-1)
    grad_qkv_weight = weight_grad(normed_first_low, grad_mixed)
    mixed_sums = column_sums(grad_mixed)
    grad_query_bias = mixed_sums[:model_width]
    grad_value_bias = mixed_sums[2 * model_width :]
    grad_normed_first = back_rows(grad_mixed, qkv_weight)
    grad_from_first, grad_first_gain, grad_first_shift = first_pull(grad_normed_first)
    grad_inputs = (grad_middle + grad_from_first).astype(jnp.bfloat16)
    all_shares = (
        lax.psum_scatter(
            grad_first_gain.astype(jnp.bfloat16), "rows", scatter_dimension=0, tiled=True
        ).astype(jnp.float32),
        lax.psum_scatter(
            grad_first_shift.astype(jnp.bfloat16), "rows", scatter_dimension=0, tiled=True
        ).astype(jnp.float32),
        lax.psum_scatter(
            grad_qkv_weight.astype(jnp.bfloat16), "rows", scatter_dimension=0, tiled=True
        ).astype(jnp.float32),
        lax.psum_scatter(
            grad_query_bias.astype(jnp.bfloat16), "rows", scatter_dimension=0, tiled=True
        ).astype(jnp.float32),
        lax.psum_scatter(
            grad_value_bias.astype(jnp.bfloat16), "rows", scatter_dimension=0, tiled=True
        ).astype(jnp.float32),
        lax.psum_scatter(
            grad_out_weight.astype(jnp.bfloat16), "rows", scatter_dimension=0, tiled=True
        ).astype(jnp.float32),
        lax.psum_scatter(
            grad_out_bias.astype(jnp.bfloat16), "rows", scatter_dimension=0, tiled=True
        ).astype(jnp.float32),
        lax.psum_scatter(
            grad_second_gain.astype(jnp.bfloat16), "rows", scatter_dimension=0, tiled=True
        ).astype(jnp.float32),
        lax.psum_scatter(
            grad_second_shift.astype(jnp.bfloat16), "rows", scatter_dimension=0, tiled=True
        ).astype(jnp.float32),
        lax.psum_scatter(
            grad_fc_weight.astype(jnp.bfloat16), "rows", scatter_dimension=0, tiled=True
        ).astype(jnp.float32),
        lax.psum_scatter(
            grad_fc_bias.astype(jnp.bfloat16), "rows", scatter_dimension=0, tiled=True
        ).astype(jnp.float32),
        lax.psum_scatter(
            grad_proj_weight.astype(jnp.bfloat16), "rows", scatter_dimension=0, tiled=True
        ).astype(jnp.float32),
        lax.psum_scatter(
            grad_proj_bias.astype(jnp.bfloat16), "rows", scatter_dimension=0, tiled=True
        ).astype(jnp.float32),
    )
    (
        grad_first_gain,
        grad_first_shift,
        grad_qkv_weight,
        grad_query_bias,
        grad_value_bias,
        grad_out_weight,
        grad_out_bias,
        grad_second_gain,
        grad_second_shift,
        grad_fc_weight,
        grad_fc_bias,
        grad_proj_weight,
        grad_proj_bias,
    ) = (
        lax.psum(all_shares[0].astype(jnp.bfloat16), "seq").astype(jnp.float32),
        lax.psum(all_shares[1].astype(jnp.bfloat16), "seq").astype(jnp.float32),
        lax.psum(all_shares[2].astype(jnp.bfloat16), "seq").astype(jnp.float32),
        lax.psum(all_shares[3].astype(jnp.bfloat16), "seq").astype(jnp.float32),
        lax.psum(all_shares[4].astype(jnp.bfloat16), "seq").astype(jnp.float32),
        lax.psum(all_shares[5].astype(jnp.bfloat16), "seq").astype(jnp.float32),
        lax.psum(all_shares[6].astype(jnp.bfloat16), "seq").astype(jnp.float32),
        lax.psum(all_shares[7].astype(jnp.bfloat16), "seq").astype(jnp.float32),
        lax.psum(all_shares[8].astype(jnp.bfloat16), "seq").astype(jnp.float32),
        lax.psum(all_shares[9].astype(jnp.bfloat16), "seq").astype(jnp.float32),
        lax.psum(all_shares[10].astype(jnp.bfloat16), "seq").astype(jnp.float32),
        lax.psum(all_shares[11].astype(jnp.bfloat16), "seq").astype(jnp.float32),
        lax.psum(all_shares[12].astype(jnp.bfloat16), "seq").astype(jnp.float32),
    )
    return (
        output,
        grad_inputs,
        grad_first_gain,
        grad_first_shift,
        grad_qkv_weight,
        grad_query_bias,
        grad_value_bias,
        grad_out_weight,
        grad_out_bias,
        grad_second_gain,
        grad_second_shift,
        grad_fc_weight,
        grad_fc_bias,
        grad_proj_weight,
        grad_proj_bias,
    )


def local_rows(
    inputs,
    doc_ids,
    first_gain,
    first_shift,
    qkv_weight,
    query_bias,
    value_bias,
    out_weight,
    out_bias,
    second_gain,
    second_shift,
    fc_weight,
    fc_bias,
    proj_weight,
    proj_bias,
    cotangent,
):
    vectors = (out_bias, second_gain, second_shift, proj_bias, first_gain, first_shift, query_bias, value_bias)
    inputs_row, cot_row, mixed, attended_low, lse, start, vec_in = front(inputs, cotangent, doc_ids, vectors, qkv_weight)
    inputs_row = inputs_row.reshape(-1, inputs.shape[2])
    cot_row = cot_row.reshape(-1, inputs.shape[2])
    *results, vecs = back(
        "rc", inputs_row, attended_low, cot_row, mixed, lse, start, out_weight, fc_weight, proj_weight, qkv_weight, vec_in, fc_bias[None]
    )
    output, grad_inputs, qkv_share, out_share, fc_share, proj_share, *small = tail(vecs, *results)
    small = [v.reshape(-1) for v in small]
    return (
        output,
        grad_inputs,
        small[4],
        small[5],
        qkv_share,
        small[6],
        small[7],
        out_share,
        small[2],
        small[0],
        small[1],
        fc_share,
        small[8],
        proj_share,
        small[3],
    )


def solution(mesh):
    in_specs = (
        P("rows", "seq", None),
        P("rows", "seq"),
        P(),
        P(),
        P(),
        P(),
        P(),
        P(),
        P(),
        P(),
        P(),
        P(),
        P(),
        P(),
        P(),
        P("rows", "seq", None),
    )
    out_specs = (
        P("rows", "seq", None),
        P("rows", "seq", None),
        P("rows"),
        P("rows"),
        P("rows", None),
        P("rows"),
        P("rows"),
        P("rows", None),
        P("rows"),
        P("rows"),
        P("rows"),
        P("rows", None),
        P("rows"),
        P("rows", None),
        P("rows"),
    )
    sizes = dict(mesh.shape)

    def chosen(inputs, *others):
        whole_rows = sizes["seq"] == 2 and sizes["rows"] == 16 and inputs.shape[0] == 2
        return (local_rows if whole_rows else local)(inputs, *others)

    return jax.shard_map(chosen, mesh=mesh, in_specs=in_specs, out_specs=out_specs, check_vma=False)
```

```python
import functools
import math

import jax
import jax.numpy as jnp
from jax import lax
from jax.experimental import pallas as pl
from jax.experimental.pallas import tpu as pltpu
from jax.sharding import PartitionSpec as P

H = 12
HD = 64
LAYERS = 12


epsilon = 1e-05
masked_value = -1e30


def layer_norm(values, norm_gain, norm_bias):
    row_mean = jnp.mean(values, axis=-1, keepdims=True)
    centred = values - row_mean
    variance = jnp.mean(centred * centred, axis=-1, keepdims=True)
    return centred * lax.rsqrt(variance + epsilon) * norm_gain + norm_bias


def gelu_tanh(values):
    return jax.nn.gelu(values, approximate=True)


def matmul_rows(left_side, weight):
    flat_rows = left_side.reshape(-1, left_side.shape[-1])
    result = jnp.dot(flat_rows, weight, preferred_element_type=jnp.float32)
    return result.reshape(left_side.shape[:-1] + (weight.shape[1],))


def back_rows(grads_low, weight):
    flat_rows = grads_low.reshape(-1, grads_low.shape[-1])
    result = jnp.einsum("nm,km->nk", flat_rows, weight, preferred_element_type=jnp.float32)
    return result.reshape(grads_low.shape[:-1] + (weight.shape[0],))


def weight_grad(left_side, right_side):
    left_flat = left_side.reshape(-1, left_side.shape[-1])
    right_flat = right_side.reshape(-1, right_side.shape[-1])
    return jnp.einsum("nk,nm->km", left_flat, right_flat, preferred_element_type=jnp.float32)


def column_sums(values):
    return jnp.sum(values.astype(jnp.float32), axis=(0, 1))


def visible(query_pos, query_doc, key_pos, key_doc):
    causal = key_pos[None, None, :] <= query_pos[None, :, None]
    same_doc = key_doc[:, None, :] == query_doc[:, :, None]
    return (causal & same_doc)[:, None]


def split_heads(kv_part):
    rows_here, key_count = (kv_part.shape[0], kv_part.shape[1])
    model_width = H * HD
    key_heads = kv_part[..., :model_width].reshape(rows_here, key_count, H, HD)
    return (key_heads, rows_here, key_count)


def scaled_scores(query_heads, key_heads, allowed):
    raw_scores = jnp.einsum(
        "rqhd,rkhd->rhqk", query_heads, key_heads, preferred_element_type=jnp.float32
    )
    return jnp.where(allowed, raw_scores * HD ** (-0.5), masked_value)


def guarded(folder, query_pos, query_doc):

    def update(totals, portion, offset):
        doc_part = portion[1]
        early_enough = offset <= query_pos[-1]
        doc_meets = jnp.any(jnp.max(doc_part, axis=1) >= jnp.min(query_doc, axis=1))
        return lax.cond(
            early_enough & doc_meets,
            lambda carried: folder(carried, portion, offset),
            lambda carried: carried,
            totals,
        )

    return update


def stats_update(query_heads, query_pos, query_doc):

    def update(totals, portion, offset):
        running_top, row_mass = totals
        kv_part, doc_part = portion
        key_heads, rows_here, key_count = split_heads(kv_part)
        key_pos = jnp.arange(key_count, dtype=jnp.int32)
        allowed = visible(query_pos, query_doc, key_pos, doc_part)
        scores = scaled_scores(query_heads, key_heads, allowed)
        new_top = jnp.maximum(running_top, jnp.max(scores, axis=-1))
        weights = jnp.where(allowed, jnp.exp(scores - new_top[..., None]), 0.0)
        row_mass = jnp.sum(weights, axis=-1)
        return (new_top, row_mass)

    return guarded(update, query_pos, query_doc)


def output_update(query_heads, query_pos, query_doc, running_top, row_mass):

    def update(totals, portion, offset):
        kv_part, doc_part = portion
        key_heads, rows_here, key_count = split_heads(kv_part)
        value_heads = kv_part[..., H * HD :].reshape(rows_here, key_count, H, HD)
        key_pos = jnp.arange(key_count, dtype=jnp.int32)
        allowed = visible(query_pos, query_doc, key_pos, doc_part)
        scores = scaled_scores(query_heads, key_heads, allowed)
        attn_probs = (
            jnp.where(allowed, jnp.exp(scores - running_top[..., None]), 0.0) / row_mass[..., None]
        )
        result = jnp.einsum(
            "rhqk,rkhd->rqhd",
            attn_probs.astype(jnp.bfloat16),
            value_heads,
            preferred_element_type=jnp.float32,
        )
        return result.reshape(totals.shape)

    return guarded(update, query_pos, query_doc)


def backward_update(
    query_heads, grad_heads, query_pos, query_doc, running_top, row_mass, row_delta
):

    def update(totals, portion, offset):
        grad_query, kv_grads = totals
        kv_part, doc_part = portion
        key_heads, rows_here, key_count = split_heads(kv_part)
        value_heads = kv_part[..., H * HD :].reshape(rows_here, key_count, H, HD)
        key_pos = jnp.arange(key_count, dtype=jnp.int32)
        allowed = visible(query_pos, query_doc, key_pos, doc_part)
        scores = scaled_scores(query_heads, key_heads, allowed)
        attn_probs = (
            jnp.where(allowed, jnp.exp(scores - running_top[..., None]), 0.0) / row_mass[..., None]
        )
        grad_probs = jnp.einsum(
            "rqhd,rkhd->rhqk", grad_heads, value_heads, preferred_element_type=jnp.float32
        )
        grad_scores = (attn_probs * (grad_probs - row_delta[..., None]) * HD ** (-0.5)).astype(
            jnp.bfloat16
        )
        query_part = jnp.einsum(
            "rhqk,rkhd->rqhd", grad_scores, key_heads, preferred_element_type=jnp.float32
        )
        grad_query = query_part.reshape(grad_query.shape)
        key_part = jnp.einsum(
            "rhqk,rqhd->rkhd", grad_scores, query_heads, preferred_element_type=jnp.float32
        )
        value_part = jnp.einsum(
            "rhqk,rqhd->rkhd",
            attn_probs.astype(jnp.bfloat16),
            grad_heads,
            preferred_element_type=jnp.float32,
        )
        piece_grads = jnp.concatenate(
            [
                key_part.reshape(rows_here, key_count, H * HD),
                value_part.reshape(rows_here, key_count, H * HD),
            ],
            axis=-1,
        )
        kv_grads = piece_grads
        return (grad_query, kv_grads)

    return guarded(update, query_pos, query_doc)


BF=jnp.bfloat16; F32=jnp.float32
NT=(((1,),(1,)),((),()))
NN=(((1,),(0,)),((),()))
C2=0.125*math.log2(math.e)
QB=256
def dot(a,b,dn=NN): return lax.dot_general(a,b,dn,preferred_element_type=F32)
def half_mask(x,h):
    lane=lax.broadcasted_iota(jnp.int32,x.shape,1)
    return jnp.where((lane<64) if h==0 else (lane>=64), x, jnp.zeros_like(x))
TN=(((0,),(0,)),((),()))
D=768
SC=12**-0.5
EPS=1e-5
G0=math.sqrt(2/math.pi); G1=0.044715
TB=256
def ln_stats(x):
    mean=jnp.mean(x,axis=-1,keepdims=True); c=x-mean
    var=jnp.mean(c*c,axis=-1,keepdims=True)
    r=lax.rsqrt(var+EPS)
    return c*r, r
def step_first(x_ref,att_ref,cot_ref,outw_ref,outb,gain,shift,mid,n2,gb2,b2,e):
    T=mid.shape[0]
    for t in range(0,T,TB):
        sl=slice(t,t+TB)
        m=x_ref[sl].astype(F32)+(dot(att_ref[sl],outw_ref[...])+outb[...])*SC
        mid[sl]=m
        xh,_=ln_stats(m)
        n2[sl]=(xh*gain[...]+shift[...]).astype(BF)
        gb2[sl]=(cot_ref[sl].astype(F32)*SC).astype(BF)
        b2[sl]=jnp.zeros((TB,D),F32); e[sl]=jnp.zeros((TB,D),F32)
def gelu_both(h):
    h2=h*h
    t=jnp.tanh(h*(G0+(G0*G1)*h2))
    half=0.5*(1+t)
    act=h*half
    dg=half+act*(1-t)*(G0+(3*G0*G1)*h2)
    return act,dg
def step_ff(fcw,fcb,projw,n2,gb2,acts,dhs,b2,e,gfc,gproj,gfcb,hook):
    T=n2.shape[0]
    cs=jnp.zeros((1,fcw.shape[1]),F32)
    blocks=[slice(t,t+TB) for t in range(0,T,TB)]
    first=lambda sl:(dot(n2[sl],fcw[...])+fcb[...], dot(gb2[sl],projw[...],NT))
    now=first(blocks[0])
    hook(0)
    for k,sl in enumerate(blocks):
        later=first(blocks[k+1]) if k+1<len(blocks) else None
        h,dA=now
        act,dg=gelu_both(h)
        ab=act.astype(BF); acts[sl]=ab
        dh=(dA*dg).astype(BF); dhs[sl]=dh
        cs=cs+jnp.sum(dh.astype(F32),axis=0,keepdims=True)
        b2[sl]+=dot(ab,projw[...])
        e[sl]+=dot(dh,fcw[...],NT)
        now=later
        hook(k+1)
    gfcb[...]=cs
    gproj(dot(acts[...],gb2[...],TN).astype(BF))
    hook(5)
    gfc(dot(n2[...],dhs[...],TN).astype(BF))
    hook(6)
def step_after(cot_ref,att_ref,outw_ref,projb,gain,mid,b2,e,gb2,out,gb1,do,gout,vecs,after_out):
    T=mid.shape[0]
    for t in range(0,T,TB):
        sl=slice(t,t+TB)
        out[sl]=(mid[sl]+(b2[sl]+projb[...])*SC).astype(BF)
    after_out()
    z=jnp.zeros((1,D),F32); sg=z; ss=z; sb1=z; sb2=z
    for t in range(0,T,TB):
        sl=slice(t,t+TB)
        m=mid[sl]
        xh,r=ln_stats(m)
        ee=e[sl]
        sg=sg+jnp.sum(ee*xh,axis=0,keepdims=True); ss=ss+jnp.sum(ee,axis=0,keepdims=True)
        g=ee*gain[...]
        gm=cot_ref[sl].astype(F32)+r*(g-jnp.mean(g,axis=-1,keepdims=True)-xh*jnp.mean(g*xh,axis=-1,keepdims=True))
        mid[sl]=gm
        b1=(gm*SC).astype(BF); gb1[sl]=b1
        sb1=sb1+jnp.sum(b1.astype(F32),axis=0,keepdims=True); sb2=sb2+jnp.sum(gb2[sl].astype(F32),axis=0,keepdims=True)
        do[sl]=dot(b1,outw_ref[...],NT).astype(BF)
    gout(dot(att_ref[...],gb1[...],TN).astype(BF))
    for k,v in enumerate((sg,ss,sb1,sb2)): vecs[k:k+1,:]=v
MESH=pl.DeviceIdType.MESH
CH=128
def first_seen(docs):
    T=docs.shape[1]
    place=lax.broadcasted_iota(jnp.int32,docs.shape,1)
    before=pltpu.roll(docs,1,1)
    start=jnp.where((docs!=before)&(place>0),place,0)
    sh=1
    while sh<T:
        start=jnp.maximum(start,jnp.where(place>=sh,pltpu.roll(start,sh,1),0))
        sh*=2
    return start
def build_bias_tri(start,bias,T):
    for i in range(T//QB):
        kk=(i+1)*QB; b0=i*(i+1)//2*QB
        key=lax.broadcasted_iota(jnp.int32,(kk,QB),0); qry=lax.broadcasted_iota(jnp.int32,(kk,QB),1)+i*QB
        ok=(key<=qry)&(key>=start[:,i*QB:kk])
        bias[b0:b0+kk,:]=jnp.where(ok,0.0,-1e30)
def front_kernel(inp,cot,docs,v0,v1,v2,v3,v4,v5,v6,v7,qkvw,xrow,cotrow,mixed,att,lse_ref,start_ref,vec_in,xs,wv,mx,dr,bias,oT,send,recv,loc,wsem,osem):
    step=pl.program_id(0)
    T=mx.shape[0]; half=T//2; n=half//CH
    s=lax.axis_index("seq"); r=lax.axis_index("rows")
    peer=(1-s,r)
    row=lambda k: vec_in[k:k+1,:]
    def remote(src,dst,k): return pltpu.make_async_remote_copy(src_ref=src,dst_ref=dst,send_sem=send.at[k],recv_sem=recv.at[k],device_id=peer,device_id_type=MESH)
    def x_copy(c): return remote(inp.at[1-s,pl.ds(c*CH,CH)],xs.at[s,pl.ds(c*CH,CH)],c)
    def d_copy(): return remote(docs.at[pl.ds(1-s,1)],dr.at[pl.ds(s,1)],n)
    def cot_copy(): return remote(cot.at[1-s],cotrow.at[s],n+1)
    def own(k):
        one=pl.ds(s,1)
        src,dst=((inp.at[s],xs.at[s]),(docs.at[one],dr.at[one]),(cot.at[s],cotrow.at[s]))[k]
        return pltpu.make_async_copy(src,dst,loc.at[k])
    def rows_out(h): return pltpu.make_async_copy(xs.at[h],xrow.at[h],osem.at[h])
    def mixed_out(h): return pltpu.make_async_copy(mx.at[pl.ds(h*half,half)],mixed.at[pl.ds(h*half,half)],osem.at[2+h])
    def project(h,t,size):
        xh,_=ln_stats(xs[h,pl.ds(t,size)].astype(F32))
        nb=(xh*row(4)+row(5)).astype(BF)
        at=pl.ds(pl.multiple_of(h*half+t,CH),size)
        mx[at,0:D]=(dot(nb,wv[:,0:D])+row(6)).astype(BF)
        mx[at,D:2*D]=dot(nb,wv[:,D:2*D]).astype(BF)
        mx[at,2*D:3*D]=(dot(nb,wv[:,2*D:3*D])+row(7)).astype(BF)
    @pl.when(step==0)
    def _():
        bar=pltpu.get_barrier_semaphore()
        pl.semaphore_signal(bar,inc=1,device_id=peer,device_id_type=MESH)
        own(0).start(); own(1).start()
        for k,v in enumerate((v0,v1,v2,v3,v4,v5,v6,v7)): vec_in[k:k+1,:]=v[...].reshape(1,D)
        weight=pltpu.make_async_copy(qkvw,wv,wsem)
        weight.start()
        pl.semaphore_wait(bar,1)
        d_copy().start()
        for c in range(n): x_copy(c).start()
        cot_copy().start()
        own(2).start()
        own(0).wait(); weight.wait()
        for t in range(0,half,TB): project(s,t,TB)
        own(1).wait(); d_copy().wait_recv()
        docs_row=jnp.concatenate([dr[0:1,:],dr[1:2,:]],axis=1)
        start=first_seen(docs_row)
        start_ref[...]=start
        build_bias_tri(start,bias,T)
        for c in range(n):
            x_copy(c).wait_recv()
            project(1-s,c*CH,CH)
        for h in range(2): rows_out(h).start(); mixed_out(h).start()
    @pl.when(step>0)
    def _():
        p=step-1
        cols=lambda base: pl.ds(pl.multiple_of(base+p*128,128),128)
        q=mx[:,cols(0)]; k=mx[:,cols(D)]
        vT=mx[:,cols(2*D)].astype(F32).T.astype(BF)
        queries=[half_mask(q,h) for h in range(2)]
        def scores(h,i):
            kk=(i+1)*QB; b0=i*(i+1)//2*QB
            return dot(k[:kk],queries[h][i*QB:kk],NT)*C2+bias[b0:b0+kk,:]
        jobs=[(h,i) for i in range(T//QB) for h in range(2)]
        res={}
        now=scores(*jobs[0])
        for a,(h,i) in enumerate(jobs):
            later=scores(*jobs[a+1]) if a+1<len(jobs) else None
            kk=(i+1)*QB
            top=jnp.max(now,axis=0,keepdims=True)
            probs=jnp.exp2(now-top)
            mass=jnp.sum(probs,axis=0,keepdims=True)
            part=dot(vT[h*64:(h+1)*64,:kk],probs.astype(BF))
            res[h,i]=(part/mass,top+jnp.log2(mass))
            now=later
        for (h,i),(part,lse) in res.items():
            sl=slice(i*QB,(i+1)*QB)
            oT[h*64:(h+1)*64,sl]=part; lse_ref[0,h:h+1,sl]=lse
        att[...]=oT[...].T.astype(BF)
    @pl.when(step==6)
    def _():
        for h in range(2): rows_out(h).wait(); mixed_out(h).wait()
        for c in range(n): x_copy(c).wait_send()
        d_copy().wait_send()
        cot_copy().wait(); own(2).wait()
def front(inp,cot,docs,vectors,qkvw):
    T=2*inp.shape[1]; half=T//2
    S=jax.ShapeDtypeStruct; V=pltpu.VMEM
    anyw=pl.BlockSpec(memory_space=pl.ANY)
    pos=lambda s: jnp.maximum(s-1,0)
    n=half//CH
    DMA=pltpu.SemaphoreType.DMA
    return pl.pallas_call(front_kernel,grid=(7,),
      in_specs=[anyw,anyw,anyw]+[pl.BlockSpec((D,),lambda s:(0,))]*8+[anyw],
      out_shape=(S((2,half,D),BF),S((2,half,D),BF),S((T,3*D),BF),S((T,D),BF),S((6,2,T),F32),S((1,T),jnp.int32),S((8,D),F32)),
      out_specs=(anyw,anyw,anyw,pl.BlockSpec((T,128),lambda s:(0,pos(s))),pl.BlockSpec((1,2,T),lambda s:(pos(s),0,0)),pl.BlockSpec((1,T),lambda s:(0,0)),pl.BlockSpec((8,D),lambda s:(0,0))),
      scratch_shapes=[V((2,half,D),BF),V((D,3*D),BF),V((T,3*D),BF),V((2,half),jnp.int32),V((10*QB,QB),F32),V((128,T),F32),
        DMA((n+2,)),DMA((n+2,)),DMA((3,)),DMA,DMA((4,))],
      compiler_params=pltpu.CompilerParams(vmem_limit_bytes=64<<20,collective_id=2,has_side_effects=True,dimension_semantics=("arbitrary",)),name="front")(inp,cot,docs,*vectors,qkvw)
NB=48
ZFIRST=(0, 1, 2, 3)
def add_low(a,b): return (a.astype(F32)+b.astype(F32)).astype(BF)
class Sums:
    def __init__(self,refs,sems,outs):
        (self.gf,self.gp,self.rf,self.rp,self.a,self.ap,self.b1,self.b1p,self.b2,self.b2p,self.b3,self.b3p,self.b4,self.b4p,self.vs,self.vr)=refs
        (self.cs,self.cr,self.credit,s1,r1,s2,r2,s3,r3,s4,r4,self.vss,self.vsr)=sems
        self.sem=((s1,r1),(s2,r2),(s3,r3),(s4,r4))
        self.out_qkv,self.out_ow,self.out_fc,self.out_proj=outs
        self.s=lax.axis_index("seq"); r=lax.axis_index("rows"); self.r=r
        self.core=lax.rem(r,2); self.x=lax.rem(r//2,2); self.zl=lax.rem(r//4,2); self.zh=r//8
        flip=lambda d,bit:(self.s, r+d-2*d*bit)
        self.peer=dict(c=flip(1,self.core),x=flip(2,self.x),z1=flip(4,self.zl),z2=flip(8,self.zh),y=(1-self.s,r))
    def greet(self):
        bar=pltpu.get_barrier_semaphore()
        for d in self.peer.values(): pl.semaphore_signal(bar,inc=1,device_id=d,device_id_type=MESH)
    def meet(self):
        pl.semaphore_wait(pltpu.get_barrier_semaphore(),len(self.peer))
    def copy(self,src,dst,ss,rs,to):
        return pltpu.make_async_remote_copy(src_ref=src,dst_ref=dst,send_sem=ss,recv_sem=rs,device_id=self.peer[to],device_id_type=MESH)
    def c_copy(self,kind):
        if kind=="f": return [self.copy(self.gf.at[:,1-self.core],self.rf,self.cs.at[0],self.cr.at[0],"c")]
        return [self.copy(self.gp.at[x,1-self.core],self.rp.at[:,x],self.cs.at[1+x],self.cr.at[1+x],"c") for x in range(2)]
    def c_start(self,kind,first):
        k=0 if kind=="f" else 1
        @pl.when(jnp.logical_not(first))
        def _(): pl.semaphore_wait(self.credit.at[k],1)
        for c in self.c_copy(kind): c.start()
    def c_finish(self,kind,u):
        for c in self.c_copy(kind): c.wait()
        if kind=="f":
            for i in range(8):
                self.a[u,i//4,(i//2)%2,i%2]=add_low(self.gf[i,self.core],self.rf[i])
        else:
            for t in range(4):
                for x in range(2):
                    self.ap[u//2,u%2,t,x]=add_low(self.gp[x,self.core,t],self.rp[t,x])
        if u<(7 if kind=="f" else 3):
            pl.semaphore_signal(self.credit.at[0 if kind=="f" else 1],inc=1,device_id=self.peer["c"],device_id_type=MESH)
    def part(self,kind,u,stage):
        x,zh,zl=self.x,self.zh,self.zl
        if kind=="f":
            a=self.a
            land=(self.b1,self.b2,self.b3,self.b4)[stage-1].at[u]
            if stage==4: return a.at[u,zh,zl,x],land,"y",[((u,zh,zl,x),())]
            if u in ZFIRST:
                if stage==1: return a.at[u,:,1-zl],land,"z1",[((u,i,zl,k),(i,k)) for i in range(2) for k in range(2)]
                if stage==2: return a.at[u,1-zh,zl],land,"z2",[((u,zh,zl,k),(k,)) for k in range(2)]
                return a.at[u,zh,zl,1-x],land,"x",[((u,zh,zl,x),())]
            if stage==1: return a.at[u,:,:,1-x],land,"x",[((u,i,k,x),(i,k)) for i in range(2) for k in range(2)]
            if stage==2: return a.at[u,:,1-zl,x],land,"z1",[((u,i,zl,x),(i,)) for i in range(2)]
            return a.at[u,1-zh,zl,x],land,"z2",[((u,zh,zl,x),())]
        ap=self.ap
        land=(self.b1p,self.b2p,self.b3p,self.b4p)[stage-1].at[u]
        if stage==1: return ap.at[u//2,u%2,:,1-x],land,"x",[((u//2,u%2,t,x),(t,)) for t in range(4)]
        if stage==2: return ap.at[:,1-zl,u,x],land,"z1",[((i,zl,u,x),(i,)) for i in range(2)]
        if stage==3: return ap.at[1-zh,zl,u,x],land,"z2",[((zh,zl,u,x),())]
        return ap.at[zh,zl,u,x],land,"y",[((zh,zl,u,x),())]
    def move(self,kind,u,stage):
        src,dst,to,_=self.part(kind,u,stage)
        k=u if kind=="f" else 8+u
        ss,rs=self.sem[stage-1]
        return self.copy(src,dst,ss.at[k],rs.at[k],to)
    def start(self,kind,u,stage): self.move(kind,u,stage).start()
    def finish(self,kind,u,stage):
        self.move(kind,u,stage).wait_recv()
        _,land,_,pairs=self.part(kind,u,stage)
        own=self.a if kind=="f" else self.ap
        for at,got in pairs:
            if stage<4: own[at]=add_low(own[at],land[got] if got else land[...])
            else: self.deliver(kind,u,own[at].astype(F32)+land[...].astype(F32))
        if stage<4 and not (kind=="p" and stage==1): self.start(kind,u,stage+1)
    def deliver(self,kind,u,total):
        if kind=="p": self.out_proj[u*NB:(u+1)*NB,:]=total
        elif u<4: self.out_fc[:,u*D:(u+1)*D]=total
        elif u==4: self.out_ow[...]=total
        else:
            for part in range(3):
                at=part*D+(u-5)*256
                self.out_qkv[:,at:at+256]=total[:,part*256:(part+1)*256]
    def wait_sends(self,kind,u):
        for stage in (1,2,3,4): self.move(kind,u,stage).wait_send()
    def v_copy(self,k):
        return self.copy(self.vs.at[k],self.vr.at[k],self.vss.at[k],self.vsr.at[k],("c","x","z1","z2","y")[k])
    def v_finish(self,k):
        self.v_copy(k).wait()
        self.vs[k+1]=self.vs[k]+self.vr[k]
        if k<4: self.v_copy(k+1).start()

def attn_pair(q_ref,k_ref,v_ref,do,o,lse_ref,bias,dqT,dk,dv,put,hook):
    T=q_ref.shape[0]
    hook(0)
    prod=(do.astype(F32)*o.astype(F32)).T
    kT=k_ref[...].astype(F32).T.astype(BF)
    dk[...]=jnp.zeros_like(dk); dv[...]=jnp.zeros_like(dv)
    for h in range(2):
        qh=half_mask(q_ref[...],h); doh=half_mask(do,h)
        delta=jnp.sum(prod[h*64:(h+1)*64],axis=0,keepdims=True)
        for i in range(T//QB):
            kk=(i+1)*QB; sl=slice(i*QB,kk); b0=i*(i+1)//2*QB
            s=dot(k_ref[0:kk,:],qh[sl],NT)*C2+bias[b0:b0+kk,:]
            p=jnp.exp2(s-lse_ref[0,h:h+1,sl])
            dp=dot(v_ref[0:kk,:],doh[sl],NT)
            ds=(p*(dp-delta[:,sl])).astype(BF)
            dv[0:kk,:]+=dot(p.astype(BF),doh[sl])
            dk[0:kk,:]+=dot(ds,qh[sl])
            dqT[h*64:(h+1)*64,sl]=dot(kT[h*64:(h+1)*64,:kk],ds)
        hook(h+1)
    put(0,(dqT[...].T*0.125).astype(BF))
    put(1,(dk[...]*0.125).astype(BF))
    put(2,dv[...].astype(BF))
NSTEP=12
PLAN={}
def plan(text):
    PLAN.clear()
    for line in text.strip().splitlines():
        where,what=line.split(":")
        k,q=where.split(".")
        PLAN.setdefault((int(k),int(q)),[]).extend(what.split())
plan("""
0.5: cs_p0
0.6: cs_f0
1.1: c_p0  s_p0
1.3: c_f0  s_f0
1.5: cs_p1
1.6: cs_f1
2.1: c_p1  s_p1
2.3: c_f1  s_f1
2.5: cs_p2
2.6: cs_f2
3.1: c_p2  s_p2
3.2: 1_p0
3.3: c_f2  s_f2
3.4: 1_f0
3.5: cs_p3
3.6: cs_f3
4.1: c_f3  s_f3  1_p1  c_p3  s_p3
4.2: cs_f4  1_f1
5.1: c_f4  s_f4
5.2: 1_p2  2_f0
6.1: 1_f2
6.3: cs_f5
7.2: 2_f1  1_p3  z_p0  z_p1  z_p2  z_p3  1_f3  c_f5  s_f5
8.3: cs_f6
8.4: 1_f4  2_f2
9.1: 3_f0  c_f6  s_f6
10.1: 3_f1
10.3: cs_f7  2_p0  2_f3
10.4: c_f7  s_f7  2_p1
11.0: 1_f5
11.1: 3_f2  2_p2  4_f0
11.3: 2_p3  4_f1  1_f6  3_p0  3_f3  2_f4  3_p1  v0  3_p2  2_f5  3_p3  1_f7  v1  3_f4  3_f5  2_f6  3_f6  2_f7  v2  3_f7  v3  4_f2  4_p0  4_f3  4_p1  4_p2  4_p3  4_f4  4_f5  4_f6  4_f7  v4
""")
def back_kernel(flags,*refs):
    (x,att,cot,outw,fcw,projw,q_ref,k_ref,v_ref,lse_ref,wq,wk,wv,start,vec_in,fcb,
     out_hbm,gin_hbm,out_qkv,out_ow,out_fc,out_proj,vec_out,
     n2,gb2,acts,dhs,b2,e,mid,bias,dqT,dk,dv,fcbs,vecs,
     *rest)=refs
    nsum=16
    S=Sums(rest[:nsum],rest[nsum:nsum+13],(out_qkv,out_ow,out_fc,out_proj))
    swap_s,swap_r,loc=rest[nsum+13:]
    T=mid.shape[0]; half=T//2
    step=pl.program_id(0)
    row=lambda k: vec_in.at[k:k+1]
    OUTB,G2,S2,PB,G1_,S1_=range(6)
    comm="r" in flags; comp="c" in flags
    place=S.s
    def keep_copy(src,dst,k):
        return pltpu.make_async_copy(src.at[pl.ds(place*half,half)],dst.at[place],loc.at[k])
    def give_copy(src,dst,k):
        return S.copy(src.at[pl.ds((1-place)*half,half)],dst.at[place],swap_s.at[k],swap_r.at[k],"y")
    def do(word):
        if word[0]=="v": return S.v_finish(int(word[1:]))
        name,(kind,u)=word.split("_")[0],word.split("_")[1]
        u=int(u)
        if name=="cs": S.c_start(kind,u==0)
        elif name=="c": S.c_finish(kind,u)
        elif name=="s": S.start(kind,u,1)
        elif name=="z": S.start(kind,u,2)
        else: S.finish(kind,u,int(name))
    def hook_for(steps):
        def hook(q):
            if not comm: return
            for k in steps:
                if (k,q) in PLAN:
                    @pl.when(step==k)
                    def _():
                        for word in PLAN[k,q]: do(word)
        return hook
    gf2=lambda val: S.gf.__setitem__(Ellipsis,val.reshape(8,2,NB,D))
    gp2=lambda val: S.gp.__setitem__(Ellipsis,val.reshape(2,2,4,NB,D))
    @pl.when(step==0)
    def _():
        if comm: S.greet()
        step_first(x,att,cot,outw,row(OUTB),row(G2),row(S2),mid,n2,gb2,b2,e)
        if comm: S.meet()
    @pl.when(step<4)
    def _():
        hook=hook_for(range(4))
        if comp: step_ff(fcw,fcb,projw,n2,gb2,acts,dhs,b2,e,gf2,gp2,fcbs.at[pl.ds(step,1)],hook)
        else:
            for q in range(7): hook(q)
    @pl.when(step==4)
    def _():
        hook=hook_for([4])
        hook(0)
        def after_out():
            if comm:
                keep_copy(dhs,out_hbm,0).start(); give_copy(dhs,out_hbm,0).start()
            hook(1)
        if comp:
            step_after(cot,att,outw,row(PB),row(G2),mid,b2,e,gb2,dhs,n2,acts,gf2,vecs,after_out)
        else: after_out()
        hook(2)
        if comp:
            build_bias_tri(start[...],bias,T)
            for t in range(0,T,TB):
                sl=slice(t,t+TB)
                xh,_=ln_stats(x[sl].astype(F32)); gb2[sl]=(xh*row(G1_)[...]+row(S1_)[...]).astype(BF)
                b2[sl]=jnp.zeros((TB,D),F32)
        hook(3)
    @pl.when((step>=5)&(step<11))
    def _():
        p=step-5; par=lax.rem(p,2); m=p//2
        cols=pl.ds(pl.multiple_of(p*128,128),128)
        hook=hook_for(range(5,11))
        def put(part,val):
            n2[:,pl.ds(pl.multiple_of(part*256+par*128,128),128)]=val
            if part!=1:
                vecs[pl.ds(6+part//2,1),cols]=jnp.sum(val.astype(F32),axis=0,keepdims=True)
        if comp: attn_pair(q_ref,k_ref,v_ref,acts[:,cols],att[:,cols],lse_ref,bias,dqT,dk,dv,put,hook)
        else:
            for q in range(3): hook(q)
        @pl.when(par==1)
        def _():
            if comp:
                gf2(dot(gb2[...],n2[...],TN).astype(BF))
            hook(3)
            if comp:
                for t in range(0,T,TB):
                    sl=slice(t,t+TB)
                    b2[sl]+=dot(n2[sl,0:256],wq[...],NT)+dot(n2[sl,256:512],wk[...],NT)+dot(n2[sl,512:768],wv[...],NT)
            hook(4)
    @pl.when(step==11)
    def _():
        hook=hook_for([11])
        if comm:
            keep_copy(dhs,out_hbm,0).wait(); give_copy(dhs,out_hbm,0).wait()
        if comp:
            vecs[4:6,:]=jnp.zeros((2,D),F32)
            def tok(sl):
                xh,r=ln_stats(x[sl].astype(F32)); ee=b2[sl]
                vecs[4:5,:]+=jnp.sum(ee*xh,axis=0,keepdims=True); vecs[5:6,:]+=jnp.sum(ee,axis=0,keepdims=True)
                g=ee*row(G1_)[...]
                dhs[sl]=(mid[sl]+r*(g-jnp.mean(g,axis=-1,keepdims=True)-xh*jnp.mean(g*xh,axis=-1,keepdims=True))).astype(BF)
            for q,part in enumerate((1-place,place)):
                for t in range(0,half,TB):
                    tok(pl.ds(pl.multiple_of(part*half+t,TB),TB))
                if comm: (keep_copy if q else give_copy)(dhs,gin_hbm,1).start()
                hook(q)
        elif comm:
            give_copy(dhs,gin_hbm,1).start(); hook(0); keep_copy(dhs,gin_hbm,1).start(); hook(1)
        if comm:
            S.vs[0,0:8]=vecs[...]; S.vs[0,8:12]=fcbs[...]; S.vs[0,12:16]=jnp.zeros((4,D),F32)
            S.v_copy(0).start()
            hook(2); hook(3)
            vec_out[...]=S.vs[5]
            for u in range(8): S.wait_sends("f",u)
            for u in range(4): S.wait_sends("p",u)
            keep_copy(dhs,gin_hbm,1).wait(); give_copy(dhs,gin_hbm,1).wait()
def back(flags,x,att,cot,mixed,lse,start,outw,fcw,projw,qkvw,vec_in,fcb):
    T=x.shape[0]
    once=pl.Buffered(1)
    full=lambda a,b: pl.BlockSpec((a,b),lambda s:(0,0),pipeline_mode=once)
    j=lambda s: jnp.minimum(s,3)
    p=lambda s: jnp.clip(s-5,0,5)
    m=lambda s: jnp.clip(s-5,0,5)//2
    S=jax.ShapeDtypeStruct
    V=pltpu.VMEM
    return pl.pallas_call(functools.partial(back_kernel,flags),grid=(NSTEP,),
      in_specs=[full(T,D),full(T,D),full(T,D),full(D,D),pl.BlockSpec((D,D),lambda s:(0,j(s))),pl.BlockSpec((D,D),lambda s:(j(s),0)),
        pl.BlockSpec((T,128),lambda s:(0,p(s))),pl.BlockSpec((T,128),lambda s:(0,6+p(s))),pl.BlockSpec((T,128),lambda s:(0,12+p(s))),pl.BlockSpec((1,2,T),lambda s:(p(s),0,0)),
        pl.BlockSpec((D,256),lambda s:(0,m(s))),pl.BlockSpec((D,256),lambda s:(0,3+m(s))),pl.BlockSpec((D,256),lambda s:(0,6+m(s))),
        full(1,T),full(8,D),pl.BlockSpec((1,D),lambda s:(0,j(s)))],
      out_shape=(S((2,T//2,D),BF),S((2,T//2,D),BF),S((NB,3*D),F32),S((NB,D),F32),S((NB,4*D),F32),S((4*NB,D),F32),S((16,D),F32)),
      out_specs=(pl.BlockSpec(memory_space=pl.ANY),pl.BlockSpec(memory_space=pl.ANY),full(NB,3*D),full(NB,D),full(NB,4*D),full(4*NB,D),full(16,D)),
      scratch_shapes=[V((T,D),BF)]*4+[V((T,D),F32)]*3+[V((10*QB,QB),F32),V((128,T),F32),V((T,128),F32),V((T,128),F32),V((4,D),F32),V((8,D),F32)]
        +[V((8,2,NB,D),BF),V((2,2,4,NB,D),BF),V((8,NB,D),BF),V((4,2,NB,D),BF),V((8,2,2,2,NB,D),BF),V((2,2,4,2,NB,D),BF),V((8,2,2,NB,D),BF),V((4,4,NB,D),BF),
          V((8,2,NB,D),BF),V((4,2,NB,D),BF),V((8,NB,D),BF),V((4,NB,D),BF),V((8,NB,D),BF),V((4,NB,D),BF),V((6,16,D),F32),V((5,16,D),F32)]
        +[pltpu.SemaphoreType.DMA((3,)),pltpu.SemaphoreType.DMA((3,)),pltpu.SemaphoreType.REGULAR((2,))]+[pltpu.SemaphoreType.DMA((12,))]*8+[pltpu.SemaphoreType.DMA((5,))]*2
        +[pltpu.SemaphoreType.DMA((2,))]*3,
      compiler_params=pltpu.CompilerParams(vmem_limit_bytes=64<<20,collective_id=1 if "r" in flags else None,has_side_effects=True,dimension_semantics=("arbitrary",)),name="back_"+flags)(x,att,cot,outw,fcw,projw,mixed,mixed,mixed,lse,qkvw,qkvw,qkvw,start,vec_in,fcb)
def tail_kernel(vecs,out_in,gin_in,qkv_in,ow_in,fc_in,proj_in,out,gin,qkv,ow,fc,proj,v0,v1,v2,v3,v4,v5,v6,v7,fcb):
    for a,b in ((out_in,out),(gin_in,gin),(qkv_in,qkv),(ow_in,ow),(fc_in,fc),(proj_in,proj)): b[...]=a[...]
    @pl.when(pl.program_id(0)==0)
    def _():
        r=lax.axis_index("rows")
        turned=pltpu.roll(vecs[0:8,:],lax.rem(16-r,16)*NB,1)
        for k,ref in enumerate((v0,v1,v2,v3,v4,v5,v6,v7)): ref[...]=turned[k:k+1,0:NB]
        line=pltpu.roll(jnp.broadcast_to(vecs[pl.ds(8+r//4,1),:],(8,D)),lax.rem(4-lax.rem(r,4),4)*4*NB,1)
        fcb[...]=line[0:1,0:4*NB]
def tail(vecs,*arrays):
    S=jax.ShapeDtypeStruct
    out,gin,qkv,ow,fc,proj=arrays
    small=[S((1,NB),F32)]*8+[S((1,4*NB),F32)]
    whole=lambda a: pl.BlockSpec(a.shape,lambda g:(0,0))
    halves=[pl.BlockSpec((1,)+out.shape[1:],lambda g:(g,0,0))]*2+[pl.BlockSpec((NB,a.shape[1]//2),lambda g:(0,g)) for a in (qkv,ow,fc)]+[pl.BlockSpec((2*NB,D),lambda g:(g,0))]
    return pl.pallas_call(tail_kernel,grid=(2,),
      in_specs=[whole(vecs)]+halves,
      out_shape=tuple(S(a.shape,a.dtype) for a in arrays)+tuple(small),
      out_specs=tuple(halves)+tuple(whole(a) for a in small),
      compiler_params=pltpu.CompilerParams(vmem_limit_bytes=64<<20,dimension_semantics=("arbitrary",)),
      name="tail")(vecs,*arrays)


def local(
    inputs,
    doc_ids,
    first_gain,
    first_shift,
    qkv_weight,
    query_bias,
    value_bias,
    out_weight,
    out_bias,
    second_gain,
    second_shift,
    fc_weight,
    fc_bias,
    proj_weight,
    proj_bias,
    cotangent,
):
    branch_scale = LAYERS ** (-0.5)
    rows_here, tokens_here, model_width = inputs.shape
    seq_count = lax.axis_size("seq")
    seq_place = lax.axis_index("seq")
    query_pos = seq_place * tokens_here + jnp.arange(tokens_here, dtype=jnp.int32)
    residual = inputs.astype(jnp.float32)
    normed_first, first_pull = jax.vjp(layer_norm, residual, first_gain, first_shift)
    normed_first_low = normed_first.astype(jnp.bfloat16)
    bias_row = jnp.concatenate([query_bias, jnp.zeros_like(query_bias), value_bias])
    mixed_proj = (matmul_rows(normed_first_low, qkv_weight) + bias_row).astype(jnp.bfloat16)
    query_heads = mixed_proj[..., :model_width].reshape(rows_here, tokens_here, H, HD)
    key_values = mixed_proj[..., model_width:]
    init_top = jnp.full((rows_here, H, tokens_here), masked_value, jnp.float32)
    init_mass = jnp.zeros((rows_here, H, tokens_here), jnp.float32)
    stats_fold = stats_update(query_heads, query_pos, doc_ids)
    running_top, row_mass = stats_fold(
        (init_top, init_mass),
        (
            lax.all_gather(key_values[..., :model_width], "seq", axis=1, tiled=True),
            lax.all_gather(doc_ids, "seq", axis=1, tiled=True),
        ),
        jnp.int32(0),
    )
    out_fold = output_update(query_heads, query_pos, doc_ids, running_top, row_mass)
    zero_rows = jnp.zeros((rows_here, tokens_here, model_width), jnp.float32)
    attended = out_fold(
        zero_rows,
        (
            lax.all_gather(key_values, "seq", axis=1, tiled=True),
            lax.all_gather(doc_ids, "seq", axis=1, tiled=True),
        ),
        jnp.int32(0),
    )
    attended_low = attended.astype(jnp.bfloat16)
    branch_one = matmul_rows(attended_low, out_weight) + out_bias
    middle = residual + branch_scale * branch_one
    normed_second, second_pull = jax.vjp(layer_norm, middle, second_gain, second_shift)
    normed_second_low = normed_second.astype(jnp.bfloat16)
    hidden = matmul_rows(normed_second_low, fc_weight) + fc_bias
    activated, gelu_pull = jax.vjp(gelu_tanh, hidden)
    activated_low = activated.astype(jnp.bfloat16)
    branch_two = matmul_rows(activated_low, proj_weight) + proj_bias
    output = (middle + branch_scale * branch_two).astype(jnp.bfloat16)
    grad_output = cotangent.astype(jnp.float32)
    grad_branch_two = (branch_scale * grad_output).astype(jnp.bfloat16)
    grad_proj_weight = weight_grad(activated_low, grad_branch_two)
    grad_proj_bias = column_sums(grad_branch_two)
    grad_activated = back_rows(grad_branch_two, proj_weight)
    grad_hidden = gelu_pull(grad_activated)[0].astype(jnp.bfloat16)
    grad_fc_weight = weight_grad(normed_second_low, grad_hidden)
    grad_fc_bias = column_sums(grad_hidden)
    grad_normed_second = back_rows(grad_hidden, fc_weight)
    grad_from_norm, grad_second_gain, grad_second_shift = second_pull(grad_normed_second)
    grad_middle = grad_output + grad_from_norm
    grad_branch_one = (branch_scale * grad_middle).astype(jnp.bfloat16)
    grad_out_weight = weight_grad(attended_low, grad_branch_one)
    grad_out_bias = column_sums(grad_branch_one)
    grad_attended = back_rows(grad_branch_one, out_weight).astype(jnp.bfloat16)
    grad_heads = grad_attended.reshape(rows_here, tokens_here, H, HD)
    row_delta = jnp.einsum(
        "rqhd,rqhd->rhq",
        grad_heads.astype(jnp.float32),
        attended.reshape(rows_here, tokens_here, H, HD),
    )
    back_fold = backward_update(
        query_heads, grad_heads, query_pos, doc_ids, running_top, row_mass, row_delta
    )
    back_initial = (
        jnp.zeros((rows_here, tokens_here, model_width), jnp.float32),
        jnp.zeros((rows_here, tokens_here * seq_count, 2 * model_width), jnp.float32),
    )
    grad_query, kv_grads = back_fold(
        back_initial,
        (
            lax.all_gather(key_values, "seq", axis=1, tiled=True),
            lax.all_gather(doc_ids, "seq", axis=1, tiled=True),
        ),
        jnp.int32(0),
    )
    kv_summed = lax.psum_scatter(
        kv_grads.astype(jnp.bfloat16), "seq", scatter_dimension=1, tiled=True
    )
    grad_mixed = jnp.concatenate([grad_query.astype(jnp.bfloat16), kv_summed], axis=-1)
    grad_qkv_weight = weight_grad(normed_first_low, grad_mixed)
    mixed_sums = column_sums(grad_mixed)
    grad_query_bias = mixed_sums[:model_width]
    grad_value_bias = mixed_sums[2 * model_width :]
    grad_normed_first = back_rows(grad_mixed, qkv_weight)
    grad_from_first, grad_first_gain, grad_first_shift = first_pull(grad_normed_first)
    grad_inputs = (grad_middle + grad_from_first).astype(jnp.bfloat16)
    all_shares = (
        lax.psum_scatter(
            grad_first_gain.astype(jnp.bfloat16), "rows", scatter_dimension=0, tiled=True
        ).astype(jnp.float32),
        lax.psum_scatter(
            grad_first_shift.astype(jnp.bfloat16), "rows", scatter_dimension=0, tiled=True
        ).astype(jnp.float32),
        lax.psum_scatter(
            grad_qkv_weight.astype(jnp.bfloat16), "rows", scatter_dimension=0, tiled=True
        ).astype(jnp.float32),
        lax.psum_scatter(
            grad_query_bias.astype(jnp.bfloat16), "rows", scatter_dimension=0, tiled=True
        ).astype(jnp.float32),
        lax.psum_scatter(
            grad_value_bias.astype(jnp.bfloat16), "rows", scatter_dimension=0, tiled=True
        ).astype(jnp.float32),
        lax.psum_scatter(
            grad_out_weight.astype(jnp.bfloat16), "rows", scatter_dimension=0, tiled=True
        ).astype(jnp.float32),
        lax.psum_scatter(
            grad_out_bias.astype(jnp.bfloat16), "rows", scatter_dimension=0, tiled=True
        ).astype(jnp.float32),
        lax.psum_scatter(
            grad_second_gain.astype(jnp.bfloat16), "rows", scatter_dimension=0, tiled=True
        ).astype(jnp.float32),
        lax.psum_scatter(
            grad_second_shift.astype(jnp.bfloat16), "rows", scatter_dimension=0, tiled=True
        ).astype(jnp.float32),
        lax.psum_scatter(
            grad_fc_weight.astype(jnp.bfloat16), "rows", scatter_dimension=0, tiled=True
        ).astype(jnp.float32),
        lax.psum_scatter(
            grad_fc_bias.astype(jnp.bfloat16), "rows", scatter_dimension=0, tiled=True
        ).astype(jnp.float32),
        lax.psum_scatter(
            grad_proj_weight.astype(jnp.bfloat16), "rows", scatter_dimension=0, tiled=True
        ).astype(jnp.float32),
        lax.psum_scatter(
            grad_proj_bias.astype(jnp.bfloat16), "rows", scatter_dimension=0, tiled=True
        ).astype(jnp.float32),
    )
    (
        grad_first_gain,
        grad_first_shift,
        grad_qkv_weight,
        grad_query_bias,
        grad_value_bias,
        grad_out_weight,
        grad_out_bias,
        grad_second_gain,
        grad_second_shift,
        grad_fc_weight,
        grad_fc_bias,
        grad_proj_weight,
        grad_proj_bias,
    ) = (
        lax.psum(all_shares[0].astype(jnp.bfloat16), "seq").astype(jnp.float32),
        lax.psum(all_shares[1].astype(jnp.bfloat16), "seq").astype(jnp.float32),
        lax.psum(all_shares[2].astype(jnp.bfloat16), "seq").astype(jnp.float32),
        lax.psum(all_shares[3].astype(jnp.bfloat16), "seq").astype(jnp.float32),
        lax.psum(all_shares[4].astype(jnp.bfloat16), "seq").astype(jnp.float32),
        lax.psum(all_shares[5].astype(jnp.bfloat16), "seq").astype(jnp.float32),
        lax.psum(all_shares[6].astype(jnp.bfloat16), "seq").astype(jnp.float32),
        lax.psum(all_shares[7].astype(jnp.bfloat16), "seq").astype(jnp.float32),
        lax.psum(all_shares[8].astype(jnp.bfloat16), "seq").astype(jnp.float32),
        lax.psum(all_shares[9].astype(jnp.bfloat16), "seq").astype(jnp.float32),
        lax.psum(all_shares[10].astype(jnp.bfloat16), "seq").astype(jnp.float32),
        lax.psum(all_shares[11].astype(jnp.bfloat16), "seq").astype(jnp.float32),
        lax.psum(all_shares[12].astype(jnp.bfloat16), "seq").astype(jnp.float32),
    )
    return (
        output,
        grad_inputs,
        grad_first_gain,
        grad_first_shift,
        grad_qkv_weight,
        grad_query_bias,
        grad_value_bias,
        grad_out_weight,
        grad_out_bias,
        grad_second_gain,
        grad_second_shift,
        grad_fc_weight,
        grad_fc_bias,
        grad_proj_weight,
        grad_proj_bias,
    )


def local_rows(
    inputs,
    doc_ids,
    first_gain,
    first_shift,
    qkv_weight,
    query_bias,
    value_bias,
    out_weight,
    out_bias,
    second_gain,
    second_shift,
    fc_weight,
    fc_bias,
    proj_weight,
    proj_bias,
    cotangent,
):
    vectors = (out_bias, second_gain, second_shift, proj_bias, first_gain, first_shift, query_bias, value_bias)
    inputs_row, cot_row, mixed, attended_low, lse, start, vec_in = front(inputs, cotangent, doc_ids, vectors, qkv_weight)
    inputs_row = inputs_row.reshape(-1, inputs.shape[2])
    cot_row = cot_row.reshape(-1, inputs.shape[2])
    *results, vecs = back(
        "rc", inputs_row, attended_low, cot_row, mixed, lse, start, out_weight, fc_weight, proj_weight, qkv_weight, vec_in, fc_bias[None]
    )
    output, grad_inputs, qkv_share, out_share, fc_share, proj_share, *small = tail(vecs, *results)
    small = [v.reshape(-1) for v in small]
    return (
        output,
        grad_inputs,
        small[4],
        small[5],
        qkv_share,
        small[6],
        small[7],
        out_share,
        small[2],
        small[0],
        small[1],
        fc_share,
        small[8],
        proj_share,
        small[3],
    )


def solution(mesh):
    in_specs = (
        P("rows", "seq", None),
        P("rows", "seq"),
        P(),
        P(),
        P(),
        P(),
        P(),
        P(),
        P(),
        P(),
        P(),
        P(),
        P(),
        P(),
        P(),
        P("rows", "seq", None),
    )
    out_specs = (
        P("rows", "seq", None),
        P("rows", "seq", None),
        P("rows"),
        P("rows"),
        P("rows", None),
        P("rows"),
        P("rows"),
        P("rows", None),
        P("rows"),
        P("rows"),
        P("rows"),
        P("rows", None),
        P("rows"),
        P("rows", None),
        P("rows"),
    )
    sizes = dict(mesh.shape)

    def chosen(inputs, *others):
        whole_rows = sizes["seq"] == 2 and sizes["rows"] == 16 and inputs.shape[0] == 2
        return (local_rows if whole_rows else local)(inputs, *others)

    return jax.shard_map(chosen, mesh=mesh, in_specs=in_specs, out_specs=out_specs, check_vma=False)
```
